32 devices in a mesh: fsdp: 4 (over y, x), ctx: 2 (over core), tp: 4 (over z).
Axes of the slice: x: 2, y: 2, z: 4, core: 2. Of those that a mesh axis runs over, the one named last changes fastest.
Arguments:
- tokens: bfloat16 [12, 640, 1024], P('fsdp', 'ctx')
- lengths: int32 [12, 2], P('fsdp'), may hold values from 257 to 320, as said below
- image_count: int32 [4], P('fsdp'), may hold values from 1 to 3, as said below
- qkv_weight: bfloat16 [2, 1024, 3, 1024], P(None, 'fsdp', None, 'tp')
- qv_bias: bfloat16 [2, 2, 4, 256], P(None, None, 'tp', 'fsdp'), may hold values from -0.59765625 to 0.59765625
- out_weight: bfloat16 [2, 1024, 1024], P(None, 'tp', 'fsdp')
- out_bias: bfloat16 [2, 1024], P(None, 'fsdp'), may hold values from -1.796875 to 1.796875
- up_weight: bfloat16 [2, 1024, 4096], P(None, 'fsdp', 'tp')
- up_bias: bfloat16 [2, 4, 1024], P(None, 'tp', 'fsdp'), may hold values from -1.796875 to 1.796875
- down_weight: bfloat16 [2, 4096, 1024], P(None, 'tp', 'fsdp')
- down_bias: bfloat16 [2, 1024], P(None, 'fsdp'), may hold values from -1.796875 to 1.796875
- gain_one: bfloat16 [2, 1024], P(None, 'fsdp'), may hold values from 0.5 to 1.5
- gain_two: bfloat16 [2, 1024], P(None, 'fsdp'), may hold values from 0.5 to 1.5
- cotangent: bfloat16 [12, 640, 1024], P('fsdp', 'ctx')
Outputs:
- output: bfloat16 [12, 640, 1024], P('fsdp', 'ctx')
- input_grad: bfloat16 [12, 640, 1024], P('fsdp', 'ctx')
- qkv_weight_grad: float32 [2, 1024, 3, 1024], P(None, 'fsdp', None, 'tp')
- qv_bias_grad: float32 [2, 2, 4, 256], P(None, None, 'tp', 'fsdp')
- out_weight_grad: float32 [2, 1024, 1024], P(None, 'tp', 'fsdp')
- out_bias_grad: float32 [2, 1024], P(None, 'fsdp')
- up_weight_grad: float32 [2, 1024, 4096], P(None, 'fsdp', 'tp')
- up_bias_grad: float32 [2, 4, 1024], P(None, 'tp', 'fsdp')
- down_weight_grad: float32 [2, 4096, 1024], P(None, 'tp', 'fsdp')
- down_bias_grad: float32 [2, 1024], P(None, 'fsdp')
- gain_one_grad: float32 [2, 1024], P(None, 'fsdp')
- gain_two_grad: float32 [2, 1024], P(None, 'fsdp')
The draws below stay inside these ranges and needn't reach their ends.
Inputs may be any that keep to these rules, and one draw needn't show every extreme that they name: `lengths`: in each image one index of ctx, drawn from the seed, holds exactly 320 tokens; the other indices share the remaining 577 - 320 tokens as evenly as possible; each image's counts sum to 577. Slots 0 to image_count - 1 of an fsdp index hold images; some index holds 3.
All inputs are finite; a program needn't handle non-finite values.
Results may differ from the reference program's by a relative error of at most 0.02.
Values may be sent and summed in bfloat16 or wider, within the bound.
No kernel may reach another device: no remote copies, remote signals or barrier semaphores. Data moves between devices by JAX's collectives and lax.ppermute only.
A program may use at most 192 MiB of HBM per device.

```python
from functools import partial
import jax
import jax.numpy as jnp
from jax import lax

D = 1024
FF = 4096
HEADS = 16
HD = 64
SEQ = 577
CAP = 320
LAYERS = 2
SLOTS = 3
IMAGES = 12
ROWS = 640
GROUPS = 4
D_TP = 256
FF_TP = 1024
N_CTX = 2
N_TP = 4


def drawn_field(key, shape, deviation):
    values = jnp.clip(jax.random.normal(key, shape, jnp.float32), -4.0, 4.0)
    return (values * deviation).astype(jnp.bfloat16)


def draw_tokens(key, part):
    return drawn_field(jax.random.fold_in(key, 41), (IMAGES, ROWS, D), 1.0)


def draw_cotangent(key, part):
    return drawn_field(jax.random.fold_in(key, 43), (IMAGES, ROWS, D), 1.0)


def draw_qkv_weight(key, part):
    return drawn_field(jax.random.fold_in(key, 47), (LAYERS, D, 3, D), D ** (-0.5))


def draw_out_weight(key, part):
    return drawn_field(jax.random.fold_in(key, 53), (LAYERS, D, D), max(D // 128, 1) ** (-0.5))


def draw_up_weight(key, part):
    return drawn_field(jax.random.fold_in(key, 59), (LAYERS, D, FF), D ** (-0.5))


def draw_down_weight(key, part):
    return drawn_field(jax.random.fold_in(key, 61), (LAYERS, FF, D), FF ** (-0.5))


def draw_image_count(key, part):
    first_key, second_key = jax.random.split(jax.random.fold_in(key, 17))
    counts = jax.random.randint(first_key, (GROUPS,), 1, SLOTS + 1)
    busiest = jax.random.randint(second_key, (), 0, GROUPS)
    return jnp.where(jnp.arange(GROUPS) == busiest, SLOTS, counts).astype(jnp.int32)


def draw_lengths(key, part):
    holder = jax.random.randint(jax.random.fold_in(key, 29), (IMAGES,), 0, N_CTX)
    others = max(N_CTX - 1, 1)
    remaining = SEQ - CAP
    base_count = remaining // others
    extra_count = remaining % others
    column = jnp.arange(N_CTX)[None, :]
    after_place = column - (column > holder[:, None]).astype(jnp.int32)
    share_count = base_count + (after_place < extra_count).astype(jnp.int32)
    return jnp.where(column == holder[:, None], CAP, share_count).astype(jnp.int32)


def level_of(stream_key, dims, shards, least, high):
    factor_of = 1.0
    for position, shards_of in shards:
        steps = jax.random.uniform(jax.random.fold_in(jax.random.fold_in(stream_key, 6), position), (shards_of,), jnp.float32, least / len(shards), high / len(shards))
        factor_of = factor_of * jnp.repeat(jnp.exp(steps), dims[position] // shards_of).reshape((-1,) + (1,) * (len(dims) - 1 - position))
    return factor_of


def centred(rng, extent, scale, bound, cuts=(), kind=jnp.bfloat16):
    values = scale * jax.random.normal(rng, extent, jnp.float32)
    if cuts:
        values = values * level_of(rng, extent, cuts, -0.22, 0.18)
    return jnp.clip(values, -bound, bound).astype(kind)


def setup_inputs(seed: int = 0) -> dict:
    key_of = jax.random.split(jax.random.key(seed), 15)
    tokens = draw_tokens(jax.random.fold_in(key_of[14], 71), 0)
    lengths = draw_lengths(jax.random.fold_in(key_of[14], 71), 0)
    image_count = draw_image_count(jax.random.fold_in(key_of[14], 71), 0)
    qkv_weight = draw_qkv_weight(jax.random.fold_in(key_of[14], 71), 0)
    qv_bias = centred(key_of[4], (LAYERS, 2, N_TP, D_TP), 0.1, 0.59765625, ((2, 4), (3, 4)))
    out_weight = draw_out_weight(jax.random.fold_in(key_of[14], 71), 0)
    out_bias = centred(key_of[6], (LAYERS, D), 0.3, 1.796875, ((1, 4),))
    up_weight = draw_up_weight(jax.random.fold_in(key_of[14], 71), 0)
    up_bias = centred(key_of[8], (LAYERS, N_TP, FF_TP), 0.3, 1.796875, ((1, 4), (2, 4)))
    down_weight = draw_down_weight(jax.random.fold_in(key_of[14], 71), 0)
    down_bias = centred(key_of[10], (LAYERS, D), 0.3, 1.796875, ((1, 4),))
    gain_one = jnp.clip(1.0 + 0.1 * jax.random.normal(key_of[11], (LAYERS, D), jnp.float32), 0.5, 1.5).astype(jnp.bfloat16)
    gain_two = jnp.clip(1.0 + 0.1 * jax.random.normal(key_of[12], (LAYERS, D), jnp.float32), 0.5, 1.5).astype(jnp.bfloat16)
    cotangent = draw_cotangent(jax.random.fold_in(key_of[14], 71), 0)
    return {"tokens": tokens, "lengths": lengths, "image_count": image_count, "qkv_weight": qkv_weight, "qv_bias": qv_bias, "out_weight": out_weight, "out_bias": out_bias, "up_weight": up_weight, "up_bias": up_bias, "down_weight": down_weight, "down_bias": down_bias, "gain_one": gain_one, "gain_two": gain_two, "cotangent": cotangent}


@jax.custom_vjp
def low(v):
    return lax.optimization_barrier(v.astype(jnp.bfloat16)).astype(jnp.float32)

@jax.custom_vjp
def low_back(v):
    return v

def low_keep(v):
    return (low(v), None)

def low_pass(kept, grad):
    return (grad,)

def back_keep(v):
    return (v, None)

def back_low(kept, grad):
    return (low(grad),)
low.defvjp(low_keep, low_pass)
low_back.defvjp(back_keep, back_low)

def layer_norm(vectors, scaling):
    centre = vectors - lax.optimization_barrier(jnp.mean(vectors, axis=-1, keepdims=True))
    spread = lax.optimization_barrier(jnp.mean(centre * centre, axis=-1, keepdims=True))
    return centre * lax.rsqrt(spread + 1e-06) * scaling

def gelu_exact(values):
    return 0.5 * values * (1.0 + lax.erf(values * 0.7071067811865476))

def attend(block_items):
    queries, all_keys, values, valid = block_items
    highest = lax.Precision.HIGHEST
    scores = low_back(jnp.einsum('qhd,khd->hqk', queries, all_keys, precision=highest) * HD ** (-0.5))
    scores = jnp.where(valid[None, None, :], scores, -1000000000.0)
    highest_score = lax.optimization_barrier(jnp.max(scores, axis=-1, keepdims=True))
    exponent = jnp.exp(scores - highest_score)
    probs = low(exponent / lax.optimization_barrier(jnp.sum(exponent, axis=-1, keepdims=True)))
    return low_back(low(jnp.einsum('hqk,khd->qhd', probs, values, precision=highest)))

def forward(inputs, params, key_valid, row_mask):
    qkv_matrix, qv_shift, out_matrix, out_shift, up_matrix, up_shift, down_matrix, down_shift, gain_first, gain_second = params
    highest = lax.Precision.HIGHEST
    images, row_count, features = inputs.shape
    head_shape = (images, row_count, HEADS, HD)
    stream = inputs
    for layer_index in range(LAYERS):
        normed = low(layer_norm(stream, gain_first[layer_index]))
        project = jnp.einsum('icd,dke->icke', normed, qkv_matrix[layer_index], precision=highest)
        queries = low_back(low(project[:, :, 0] + qv_shift[layer_index, 0].reshape(features)))
        all_keys = low_back(low(project[:, :, 1]))
        values = low_back(low(project[:, :, 2] + qv_shift[layer_index, 1].reshape(features)))
        mixed = lax.map(jax.checkpoint(attend), (queries.reshape(head_shape), all_keys.reshape(head_shape), values.reshape(head_shape), key_valid))
        mixed = mixed.reshape(images, row_count, features)
        branch = low_back(jnp.einsum('ice,ed->icd', mixed, out_matrix[layer_index], precision=highest) + out_shift[layer_index])
        middle = stream + branch
        normed_b = low(layer_norm(middle, gain_second[layer_index]))
        hidden = low_back(jnp.einsum('icd,df->icf', normed_b, up_matrix[layer_index], precision=highest) + up_shift[layer_index].reshape(FF))
        active = low(gelu_exact(hidden))
        branch_b = low_back(jnp.einsum('icf,fd->icd', active, down_matrix[layer_index], precision=highest) + down_shift[layer_index])
        stream = middle + branch_b
    return stream * row_mask[:, :, None]

def reference(tokens, lengths, image_count, qkv_weight, qv_bias, out_weight, out_bias, up_weight, up_bias, down_weight, down_bias, gain_one, gain_two, cotangent):
    images, row_count, features = tokens.shape
    positions = jnp.arange(CAP)
    key_valid = (positions[None, None, :] < lengths[:, :, None]).reshape(images, row_count)
    slot_index = jnp.arange(images) % SLOTS
    owner_index = jnp.arange(images) // SLOTS
    occupied = slot_index < image_count[owner_index]
    row_mask = (key_valid & occupied[:, None]).astype(jnp.float32)
    params = tuple((array.astype(jnp.float32) for array in (qkv_weight, qv_bias, out_weight, out_bias, up_weight, up_bias, down_weight, down_bias, gain_one, gain_two)))
    output, pullback = jax.vjp(partial(forward, key_valid=key_valid, row_mask=row_mask), tokens.astype(jnp.float32), params)
    input_grad, grads = pullback(cotangent.astype(jnp.float32))
    return (output.astype(jnp.bfloat16), input_grad.astype(jnp.bfloat16), grads[0], grads[1], grads[2], grads[3], grads[4], grads[5], grads[6], grads[7], grads[8], grads[9])
```

```python
import jax
import jax.numpy as jnp
from jax import lax
from jax.sharding import PartitionSpec as P

HD = 64
SEQ = 577
BF = jnp.bfloat16
F32 = jnp.float32


def layer_norm(vectors, scaling):
    centre = vectors - jnp.mean(vectors, axis=-1, keepdims=True)
    spread = jnp.mean(centre * centre, axis=-1, keepdims=True)
    return centre * lax.rsqrt(spread + 1e-06) * scaling


def gelu_exact(values):
    return 0.5 * values * (1.0 + lax.erf(values * 0.7071067811865476))


X_PAIRS = [(0, 1), (1, 0), (2, 3), (3, 2)]
Y_PAIRS = [(0, 2), (2, 0), (1, 3), (3, 1)]


def square():
    return lax.axis_size("fsdp") == 4


def reorder(values):
    if not square():
        return values
    place = lax.axis_index("fsdp")
    lead = values.shape[:-1]
    blocks = values.reshape(lead + (2, 2, values.shape[-1] // 4))
    blocks = jnp.where(place % 2 == 1, blocks[..., :, ::-1, :], blocks)
    blocks = jnp.where(place >= 2, blocks[..., ::-1, :, :], blocks)
    return blocks.reshape(values.shape)


def send_x(values):
    return lax.ppermute(values, "fsdp", X_PAIRS)


def send_y(values):
    return lax.ppermute(values, "fsdp", Y_PAIRS)


def swap(values):
    return lax.ppermute(values, "ctx", [(0, 1), (1, 0)])


def both_cores(partial_sum):
    low = partial_sum.astype(BF)
    return low.astype(F32) + swap(low).astype(F32)


def gather_rows(shard):
    if not square():
        return lax.all_gather(shard, "fsdp", axis=0, tiled=True)
    half = shard.shape[0] // 2
    from_x, from_y = send_x(shard), send_y(shard)
    far_a, far_b = send_y(from_x[:half]), send_x(from_y[half:])
    return jnp.concatenate([shard, from_x, from_y, far_a, far_b], axis=0)


def scatter_rows(full):
    if not square():
        return lax.psum_scatter(full.astype(BF), "fsdp", scatter_dimension=0, tiled=True).astype(F32)
    rows = full.shape[0] // 4
    half = rows // 2
    own, to_x, to_y, far = [full[k * rows : (k + 1) * rows] for k in range(4)]
    first = send_x(jnp.concatenate([to_x[:half], far[:half]]).astype(BF)).astype(F32)
    second = send_y(jnp.concatenate([to_y[half:], far[half:]]).astype(BF)).astype(F32)
    own_a = own[:half] + first[:half]
    own_b = own[half:] + second[:half]
    pass_y = (to_y[:half] + first[half:]).astype(BF)
    pass_x = (to_x[half:] + second[half:]).astype(BF)
    own_a = own_a + send_y(pass_y).astype(F32)
    own_b = own_b + send_x(pass_x).astype(F32)
    return jnp.concatenate([own_a, own_b])


def gather_matrix(shard, place):
    rows, groups, columns = shard.shape
    half = lax.dynamic_index_in_dim(shard.reshape(rows, groups, 2, columns // 2), place, 2, keepdims=False)
    along = lax.all_gather(half, "tp", axis=0)
    along = jnp.transpose(along, (1, 2, 0, 3)).reshape(rows, -1)
    return gather_rows(along)


def scatter_matrix(grad, groups, place):
    count = lax.axis_size("tp")
    kept = scatter_rows(grad).astype(BF)
    rows = kept.shape[0]
    kept = jnp.transpose(kept.reshape(rows, groups, count, -1), (2, 0, 1, 3))
    own = lax.psum_scatter(kept, "tp", scatter_dimension=0, tiled=False)
    other = swap(own)
    low = jnp.where(place == 0, own, other)
    high = jnp.where(place == 0, other, own)
    return jnp.concatenate([low, high], axis=-1).astype(F32)


def heads_of(values):
    return values.reshape(values.shape[0], -1, HD)


def masked_scores(queries, keys, key_valid):
    scores = jnp.einsum("qhd,khd->hqk", queries, keys, preferred_element_type=F32) * HD ** (-0.5)
    return jnp.where(key_valid, scores, -1000000000.0)


def mm(left, right):
    return jnp.dot(left, right, preferred_element_type=F32)


def mm_nt(left, right):
    return lax.dot_general(left, right, (((1,), (1,)), ((), ())), preferred_element_type=F32)


def mm_tn(left, right):
    return lax.dot_general(left, right, (((0,), (0,)), ((), ())), preferred_element_type=F32)


def forward_layer(stream, weights, vectors, key_valid):
    qkv, out, up, down = weights
    shift_q, shift_v, out_shift, up_shift, down_shift, gain_first, gain_second = vectors
    normed = layer_norm(stream, gain_first).astype(BF)
    project = mm(normed, qkv)
    width = project.shape[1] // 3
    queries = heads_of((project[:, :width] + shift_q).astype(BF))
    keys = heads_of(project[:, width : 2 * width].astype(BF))
    values = heads_of((project[:, 2 * width :] + shift_v).astype(BF))
    scores = masked_scores(queries, keys, key_valid)
    highest = jnp.max(scores, axis=-1, keepdims=True)
    exponent = jnp.exp(scores - highest)
    denominator = jnp.sum(exponent, axis=-1, keepdims=True)
    probs = (exponent / denominator).astype(BF)
    log_total = highest + jnp.log(denominator)
    mixed = jnp.einsum("hqk,khd->qhd", probs, values, preferred_element_type=F32).astype(BF)
    mixed = mixed.reshape(stream.shape[0], width)
    middle = stream + both_cores(mm_nt(mixed, out)) + out_shift
    normed_b = layer_norm(middle, gain_second).astype(BF)
    hidden = mm(normed_b, up) + up_shift
    active = gelu_exact(hidden).astype(BF)
    following = middle + both_cores(mm_nt(active, down)) + down_shift
    return following, (stream, normed, queries, keys, values, log_total, mixed, middle, normed_b, hidden, active)


def backward_layer(gradient, saved, weights, vectors, key_valid, emit):
    qkv, out, up, down = weights
    gain_first, gain_second = vectors[5:]
    stream, normed, queries, keys, values, log_total, mixed, middle, normed_b, hidden, active = saved
    total = lambda array: jnp.sum(array.astype(F32), axis=0)
    grad_low = gradient.astype(BF)
    emit("down", mm_tn(grad_low, active))
    delta_hidden = jax.vjp(gelu_exact, hidden)[1](mm(grad_low, down))[0].astype(BF)
    emit("up", mm_tn(normed_b, delta_hidden))
    delta_normed_b = both_cores(mm_nt(delta_hidden, up))
    back_middle, delta_gain_second = jax.vjp(layer_norm, middle, gain_second)[1](delta_normed_b)
    grad_middle = gradient + back_middle
    grad_attend = grad_middle.astype(BF)
    emit("out", mm_tn(grad_attend, mixed))
    delta_mixed = heads_of(mm(grad_attend, out).astype(BF))
    probs = jnp.exp(masked_scores(queries, keys, key_valid) - log_total)
    delta_values = jnp.einsum("hqk,qhd->khd", probs.astype(BF), delta_mixed, preferred_element_type=F32).astype(BF)
    delta_probs = jnp.einsum("qhd,khd->hqk", delta_mixed, values, preferred_element_type=F32)
    inner = jnp.sum(probs * delta_probs, axis=-1, keepdims=True)
    delta_scores = (probs * (delta_probs - inner)).astype(BF)
    scale = HD ** (-0.5)
    delta_queries = (jnp.einsum("hqk,khd->qhd", delta_scores, keys, preferred_element_type=F32) * scale).astype(BF)
    delta_keys = (jnp.einsum("hqk,qhd->khd", delta_scores, queries, preferred_element_type=F32) * scale).astype(BF)
    flat = [piece.reshape(stream.shape[0], -1) for piece in (delta_queries, delta_keys, delta_values)]
    delta_project = jnp.concatenate(flat, axis=1)
    emit("qkv", mm_tn(normed, delta_project))
    delta_normed = both_cores(mm_nt(delta_project, qkv))
    back_stream, delta_gain_first = jax.vjp(layer_norm, stream, gain_first)[1](delta_normed)
    sums = (
        total(flat[0]),
        total(flat[2]),
        total(grad_attend),
        total(delta_hidden),
        total(grad_low),
        delta_gain_first,
        delta_gain_second,
    )
    return grad_middle + back_stream, sums


def shards(
    tokens,
    lengths,
    image_count,
    qkv_weight,
    qv_bias,
    out_weight,
    out_bias,
    up_weight,
    up_bias,
    down_weight,
    down_bias,
    gain_one,
    gain_two,
    cotangent,
):
    slots, capacity, features = tokens.shape
    layers = qkv_weight.shape[0]
    n_fsdp, n_tp = lax.axis_size("fsdp"), lax.axis_size("tp")
    assert lax.axis_size("ctx") == 2 and slots <= n_tp
    group, core, lane = lax.axis_index("fsdp"), lax.axis_index("ctx"), lax.axis_index("tp")
    rows = -(-SEQ // 16) * 16
    slot = jnp.minimum(lane, slots - 1)
    own_lengths = lax.dynamic_index_in_dim(lengths, slot, 0, keepdims=False)
    live = lane < jnp.minimum(image_count[0], slots)
    key_valid = (jnp.arange(rows) < SEQ)[None, None, :]
    row_mask = ((jnp.arange(rows) < SEQ) & live).astype(F32)[:, None]

    pieces = (qv_bias, up_bias, out_bias, down_bias, gain_one, gain_two)
    packed = jnp.concatenate([piece.reshape(-1) for piece in pieces])
    spread = lax.all_gather(packed, ("fsdp", "tp"), axis=0).reshape(n_fsdp, n_tp, -1)
    found, start = [], 0
    for piece in pieces:
        found.append(spread[:, :, start : start + piece.size])
        start += piece.size

    def by_core(array, count):
        array = array.reshape(n_fsdp, n_tp, layers, count, -1)
        array = jnp.transpose(array, (2, 3, 1, 0, 4)).reshape(layers, count, n_tp, 2, -1)
        return lax.dynamic_index_in_dim(array, core, 3, keepdims=False).reshape(layers, count, -1)

    def by_feature(array):
        array = array[:, 0].reshape(n_fsdp, layers, -1)
        return reorder(jnp.transpose(array, (1, 0, 2)).reshape(layers, features))

    qv_all, up_all = by_core(found[0], 2), by_core(found[1], 1)
    out_all, down_all, one_all, two_all = [by_feature(array) for array in found[2:]]
    vectors = [
        (qv_all[l, 0], qv_all[l, 1], out_all[l], up_all[l, 0], down_all[l], one_all[l], two_all[l])
        for l in range(layers)
    ]

    weights = []
    for l in range(layers):
        raw = (qkv_weight[l], out_weight[l].T[:, None], up_weight[l][:, None], down_weight[l].T[:, None])
        weights.append(tuple(gather_matrix(piece, core) for piece in raw))

    own_pair = jnp.stack([lax.dynamic_index_in_dim(a, slot, 0, keepdims=False) for a in (tokens, cotangent)])
    other_pair = swap(own_pair)
    low = jnp.where(core == 0, own_pair, other_pair)
    high = jnp.where(core == 0, other_pair, own_pair)
    image = jnp.concatenate([low, jnp.zeros_like(low)], axis=1)
    image = lax.dynamic_update_slice_in_dim(image, high, own_lengths[0], 1)[:, :rows]
    image = reorder(image).astype(F32)

    stream = image[0]
    saved = []
    for l in range(layers):
        stream, items = forward_layer(stream, weights[l], vectors[l], key_valid)
        saved.append(items)

    own_length = own_lengths[core]
    own_rows = ((jnp.arange(capacity) < own_length) & live)[:, None]

    def give_back(values):
        values = jnp.pad(reorder(values.astype(BF)), ((0, 2 * capacity - rows), (0, 0)))
        mine = lax.dynamic_slice_in_dim(values, jnp.where(core == 0, 0, own_lengths[0]), capacity, 0)
        mine = jnp.where(own_rows, mine, jnp.zeros_like(mine))
        return lax.all_gather(mine, "tp", axis=0)[:slots]

    output = give_back(stream)
    gradient = image[1] * row_mask
    grads = {}
    sums = [None] * layers
    for l in reversed(range(layers)):

        def emit(name, grad, l=l):
            grads[name, l] = scatter_matrix(grad, 3 if name == "qkv" else 1, core)

        gradient, sums[l] = backward_layer(gradient, saved[l], weights[l], vectors[l], key_valid, emit)
    input_grad = give_back(gradient)

    def from_core(array, count):
        array = array.reshape(layers, count, n_tp, 1, -1)
        mask = (jnp.arange(2) == core)[:, None]
        return jnp.where(mask, array, 0.0).reshape(layers * count, -1)

    first = (core == 0).astype(F32)
    member = lambda k: jnp.stack([sums[l][k] for l in range(layers)])
    joined = [
        from_core(jnp.stack([member(0), member(1)], axis=1), 2),
        from_core(member(3)[:, None], 1),
    ] + [reorder(member(k)) * first for k in (2, 4, 5, 6)]
    summed = lax.psum(jnp.concatenate([a.reshape(-1) for a in joined]), ("fsdp", "ctx", "tp"))
    whole, start = [], 0
    for a in joined:
        whole.append(summed[start : start + a.size])
        start += a.size
    pick = lambda a, i, axis: lax.dynamic_index_in_dim(a, i, axis, keepdims=True)
    qv_grad = pick(pick(whole[0].reshape(layers, 2, n_tp, n_fsdp, -1), lane, 2), group, 3)[:, :, :, 0]
    up_grad = pick(pick(whole[1].reshape(layers, n_tp, n_fsdp, -1), lane, 1), group, 2)[:, :, 0]
    out_shift, down_shift, one, two = [pick(a.reshape(layers, n_fsdp, -1), group, 1)[:, 0] for a in whole[2:]]

    stacked = lambda name: jnp.stack([grads[name, l] for l in range(layers)])
    qkv_grad = stacked("qkv")
    out_grad = jnp.swapaxes(stacked("out")[:, :, 0], 1, 2)
    up_w_grad = stacked("up")[:, :, 0]
    down_grad = jnp.swapaxes(stacked("down")[:, :, 0], 1, 2)
    return (
        output,
        input_grad,
        qkv_grad,
        qv_grad,
        out_grad,
        out_shift,
        up_w_grad,
        up_grad,
        down_grad,
        down_shift,
        one,
        two,
    )


def solution(mesh):
    in_specs = (
        P("fsdp", "ctx", None),
        P("fsdp", None),
        P("fsdp"),
        P(None, "fsdp", None, "tp"),
        P(None, None, "tp", "fsdp"),
        P(None, "tp", "fsdp"),
        P(None, "fsdp"),
        P(None, "fsdp", "tp"),
        P(None, "tp", "fsdp"),
        P(None, "tp", "fsdp"),
        P(None, "fsdp"),
        P(None, "fsdp"),
        P(None, "fsdp"),
        P("fsdp", "ctx", None),
    )
    out_specs = (
        P("fsdp", "ctx", None),
        P("fsdp", "ctx", None),
        P(None, "fsdp", None, "tp"),
        P(None, None, "tp", "fsdp"),
        P(None, "tp", "fsdp"),
        P(None, "fsdp"),
        P(None, "fsdp", "tp"),
        P(None, "tp", "fsdp"),
        P(None, "tp", "fsdp"),
        P(None, "fsdp"),
        P(None, "fsdp"),
        P(None, "fsdp"),
    )
    return jax.shard_map(shards, mesh=mesh, in_specs=in_specs, out_specs=out_specs, check_vma=False)
```

```python
import jax
import jax.numpy as jnp
from jax import lax
from jax.sharding import PartitionSpec as P

HD = 64
SEQ = 577
BF = jnp.bfloat16
F32 = jnp.float32


def layer_norm(vectors, scaling):
    centre = vectors - jnp.mean(vectors, axis=-1, keepdims=True)
    spread = jnp.mean(centre * centre, axis=-1, keepdims=True)
    return centre * lax.rsqrt(spread + 1e-06) * scaling


def gelu_exact(values):
    return 0.5 * values * (1.0 + lax.erf(values * 0.7071067811865476))


X_PAIRS = [(0, 1), (1, 0), (2, 3), (3, 2)]
Y_PAIRS = [(0, 2), (2, 0), (1, 3), (3, 1)]
BLOCKS = ((0, 0), (0, 1), (1, 1), (2, 0), (1, 0), (3, 0), (3, 1), (2, 1))


def square():
    return lax.axis_size("fsdp") == 4


def order_matrix(features):
    if not square():
        return None
    half = features // 8
    group = lax.axis_index("fsdp")
    starts = jnp.stack([((group ^ other) * 2 + part) * half for other, part in BLOCKS])
    natural = (starts[:, None] + jnp.arange(half)[None]).reshape(-1)
    return (jnp.arange(features)[:, None] == natural[None]).astype(BF)


def send_x(values):
    return lax.ppermute(values, "fsdp", X_PAIRS)


def send_y(values):
    return lax.ppermute(values, "fsdp", Y_PAIRS)


def swap(values):
    return lax.ppermute(values, "ctx", [(0, 1), (1, 0)])


def both_cores(partial_sum):
    low = partial_sum.astype(BF)
    return low.astype(F32) + swap(low).astype(F32)


def gather_line(shard):
    count, lane = lax.axis_size("tp"), lax.axis_index("tp")
    up_pairs = [(j, j + 1) for j in range(count - 1)]
    down_pairs = [(j + 1, j) for j in range(count - 1)]
    lower, upper = [shard], [shard]
    for step in range(count - 1):
        lower.append(lax.ppermute(lower[-1], "tp", up_pairs[step:]))
        upper.append(lax.ppermute(upper[-1], "tp", down_pairs[: count - 1 - step]))
    placed = []
    for owner in range(count):
        piece = shard
        for away in range(1, count):
            piece = jnp.where(lane == owner + away, lower[away], piece)
            piece = jnp.where(lane == owner - away, upper[away], piece)
        placed.append(piece)
    return jnp.stack(placed)


def scatter_line(full):
    count, lane = lax.axis_size("tp"), lax.axis_index("tp")
    take = lambda k: lax.dynamic_index_in_dim(full, jnp.clip(k, 0, count - 1), 0, keepdims=False)
    rising = falling = None
    for step in range(count - 1):
        to_up, to_down = take(lane + count - 1 - step), take(lane - (count - 1 - step))
        if step:
            to_up, to_down = to_up + rising, to_down + falling
        rising = lax.ppermute(to_up, "tp", [(j, j + 1) for j in range(step + 1)])
        falling = lax.ppermute(to_down, "tp", [(j + 1, j) for j in range(count - 2 - step, count - 1)])
    return (take(lane).astype(F32) + rising.astype(F32) + falling.astype(F32)).astype(BF)


def gather_features(shard):
    if not square():
        return [lax.all_gather(shard, "fsdp", axis=1, tiled=True)]
    half = shard.shape[1] // 2
    from_x, from_y = send_x(shard), send_y(shard)
    far_a, far_b = send_y(from_x[:, :half]), send_x(from_y[:, half:])
    return [shard, from_x[:, half:], from_y[:, :half], from_x[:, :half], far_a, far_b, from_y[:, half:]]


def gradient_rows(delta, values):
    if not square():
        return lax.psum_scatter(mm_tn(delta, values).astype(BF), "fsdp", scatter_dimension=1, tiled=True)
    half = values.shape[1] // 8
    to_x = mm_tn(delta, values[:, 4 * half : 6 * half]).astype(BF)
    from_x = send_x(to_x)
    to_y = mm_tn(delta, values[:, 6 * half :]).astype(BF)
    from_y = send_y(to_y)
    own_a, own_b, x_b, y_a = jnp.split(mm_tn(delta, values[:, : 4 * half]).astype(BF), 4, axis=1)
    last_a = send_y(y_a + from_x[:, half:])
    last_b = send_x(x_b + from_y[:, :half])
    add = lambda *terms: sum(term.astype(F32) for term in terms).astype(BF)
    return jnp.concatenate([add(own_a, from_x[:, :half], last_a), add(own_b, from_y[:, half:], last_b)], axis=1)


def gather_group(shards):
    count = lax.axis_size("tp")
    heights = [shard.shape[0] for shard in shards]
    along = gather_line(jnp.concatenate(shards, axis=0))
    pieces = gather_features(along.reshape(-1, along.shape[-1]))
    pieces = [piece.reshape(count, -1, piece.shape[-1]) for piece in pieces]
    result, start = [], 0
    for height in heights:
        cut = [piece[:, start : start + height].reshape(count * height, -1) for piece in pieces]
        result.append(jnp.concatenate(cut, axis=1))
        start += height
    return result


def heads_of(values):
    return values.reshape(values.shape[0], -1, HD)


def masked_scores(queries, keys, key_valid):
    scores = jnp.einsum("qhd,khd->hqk", queries, keys, preferred_element_type=F32) * HD ** (-0.5)
    return jnp.where(key_valid, scores, -1000000000.0)


def mm(left, right):
    return jnp.dot(left, right, preferred_element_type=F32)


def mm_nt(left, right):
    return lax.dot_general(left, right, (((1,), (1,)), ((), ())), preferred_element_type=F32)


def mm_tn(left, right):
    return lax.dot_general(left, right, (((0,), (0,)), ((), ())), preferred_element_type=F32)


def forward_layer(stream, weights, vectors, key_valid):
    qkv, out, up, down = weights
    shift_q, shift_v, out_shift, up_shift, down_shift, gain_first, gain_second = vectors
    normed = layer_norm(stream, gain_first).astype(BF)
    project = mm_nt(normed, qkv)
    width = project.shape[1] // 3
    tile = width // lax.axis_size("tp")
    member = lambda k: jnp.concatenate(
        [project[:, c : c + tile] for c in range(k * tile, 3 * width, 3 * tile)], axis=1
    )
    queries = heads_of((member(0) + shift_q).astype(BF))
    keys = heads_of(member(1).astype(BF))
    values = heads_of((member(2) + shift_v).astype(BF))
    scores = masked_scores(queries, keys, key_valid)
    highest = jnp.max(scores, axis=-1, keepdims=True)
    exponent = jnp.exp(scores - highest)
    denominator = jnp.sum(exponent, axis=-1, keepdims=True)
    probs = (exponent / denominator).astype(BF)
    log_total = highest + jnp.log(denominator)
    mixed = jnp.einsum("hqk,khd->qhd", probs, values, preferred_element_type=F32).astype(BF)
    mixed = mixed.reshape(stream.shape[0], width)
    middle = stream + both_cores(mm(mixed, out)) + out_shift
    normed_b = layer_norm(middle, gain_second).astype(BF)
    hidden = mm_nt(normed_b, up) + up_shift
    active = gelu_exact(hidden).astype(BF)
    following = middle + both_cores(mm(active, down)) + down_shift
    return following, (stream, normed, queries, keys, values, log_total, mixed, middle, normed_b, hidden, active)


def backward_layer(gradient, saved, weights, vectors, key_valid, emit):
    qkv, out, up, down = weights
    gain_first, gain_second = vectors[5:]
    stream, normed, queries, keys, values, log_total, mixed, middle, normed_b, hidden, active = saved
    total = lambda array: jnp.sum(array.astype(F32), axis=0)
    grad_low = gradient.astype(BF)
    emit("down", active, grad_low)
    delta_hidden = jax.vjp(gelu_exact, hidden)[1](mm_nt(grad_low, down))[0].astype(BF)
    emit("up", delta_hidden, normed_b)
    delta_normed_b = both_cores(mm(delta_hidden, up))
    back_middle, delta_gain_second = jax.vjp(layer_norm, middle, gain_second)[1](delta_normed_b)
    grad_middle = gradient + back_middle
    grad_attend = grad_middle.astype(BF)
    emit("out", mixed, grad_attend)
    delta_mixed = heads_of(mm_nt(grad_attend, out).astype(BF))
    probs = jnp.exp(masked_scores(queries, keys, key_valid) - log_total)
    delta_values = jnp.einsum("hqk,qhd->khd", probs.astype(BF), delta_mixed, preferred_element_type=F32).astype(BF)
    delta_probs = jnp.einsum("qhd,khd->hqk", delta_mixed, values, preferred_element_type=F32)
    inner = jnp.sum(probs * delta_probs, axis=-1, keepdims=True)
    delta_scores = (probs * (delta_probs - inner)).astype(BF)
    scale = HD ** (-0.5)
    delta_queries = (jnp.einsum("hqk,khd->qhd", delta_scores, keys, preferred_element_type=F32) * scale).astype(BF)
    delta_keys = (jnp.einsum("hqk,qhd->khd", delta_scores, queries, preferred_element_type=F32) * scale).astype(BF)
    flat = [piece.reshape(stream.shape[0], -1) for piece in (delta_queries, delta_keys, delta_values)]
    width = flat[0].shape[1]
    tile = width // lax.axis_size("tp")
    delta_project = jnp.concatenate([piece[:, c : c + tile] for c in range(0, width, tile) for piece in flat], axis=1)
    emit("qkv", delta_project, normed)
    delta_normed = both_cores(mm(delta_project, qkv))
    back_stream, delta_gain_first = jax.vjp(layer_norm, stream, gain_first)[1](delta_normed)
    sums = (
        total(flat[0]),
        total(flat[2]),
        total(grad_attend),
        total(delta_hidden),
        total(grad_low),
        delta_gain_first,
        delta_gain_second,
    )
    return grad_middle + back_stream, sums


def shards(
    tokens,
    lengths,
    image_count,
    qkv_weight,
    qv_bias,
    out_weight,
    out_bias,
    up_weight,
    up_bias,
    down_weight,
    down_bias,
    gain_one,
    gain_two,
    cotangent,
):
    slots, capacity, features = tokens.shape
    layers = qkv_weight.shape[0]
    n_fsdp, n_tp = lax.axis_size("fsdp"), lax.axis_size("tp")
    assert lax.axis_size("ctx") == 2 and slots <= n_tp
    group, core, lane = lax.axis_index("fsdp"), lax.axis_index("ctx"), lax.axis_index("tp")
    rows = -(-SEQ // 16) * 16
    slot = jnp.minimum(lane, slots - 1)
    own_lengths = lax.dynamic_index_in_dim(lengths, slot, 0, keepdims=False)
    live = lane < jnp.minimum(image_count[0], slots)
    key_valid = (jnp.arange(rows) < SEQ)[None, None, :]
    row_mask = ((jnp.arange(rows) < SEQ) & live).astype(F32)[:, None]
    halves = lambda array, axis: lax.dynamic_index_in_dim(
        array.reshape(array.shape[:axis] + (2, -1) + array.shape[axis + 1 :]), core, axis, keepdims=False
    )

    cut = []
    for l in range(layers):
        qkv = jnp.transpose(halves(qkv_weight[l], 2), (1, 2, 0)).reshape(-1, qkv_weight.shape[1])
        cut.append((qkv, halves(out_weight[l], 0), halves(up_weight[l], 1).T, halves(down_weight[l], 0)))
    first_qkv = gather_group([cut[0][0]])

    pieces = (qv_bias, up_bias, out_bias, down_bias, gain_one, gain_two)
    packed = jnp.concatenate([piece.reshape(1, -1) for piece in pieces], axis=1)
    if square():
        near_x, near_y = send_x(packed), send_y(packed)
        found = jnp.concatenate([packed, near_x, near_y, send_y(near_x)])
        natural = [lax.dynamic_index_in_dim(found, group ^ k, 0, keepdims=False) for k in range(4)]
        spread = jnp.stack(natural)
    else:
        spread = lax.all_gather(packed[0], "fsdp", axis=0)
    order = order_matrix(features)
    split = qv_bias.size + up_bias.size
    across = gather_line(spread[:, :split])

    def by_core(array, count):
        array = array.reshape(n_tp, n_fsdp, layers, count, -1)
        array = jnp.transpose(array, (2, 3, 0, 1, 4)).reshape(layers, count, n_tp, 2, -1)
        return lax.dynamic_index_in_dim(array, core, 3, keepdims=False).reshape(layers, count, -1)

    qv_all = by_core(across[:, :, : qv_bias.size], 2)
    up_all = by_core(across[:, :, qv_bias.size :], 1)
    by_feature = jnp.transpose(spread[:, split:].reshape(n_fsdp, 4, layers, -1), (1, 2, 0, 3)).reshape(4 * layers, features)
    if order is not None:
        by_feature = mm(by_feature, order)
    by_feature = by_feature.astype(F32).reshape(4, layers, features)
    out_all, down_all, one_all, two_all = by_feature[0], by_feature[1], by_feature[2], by_feature[3]
    vectors = [
        (qv_all[l, 0], qv_all[l, 1], out_all[l], up_all[l, 0], down_all[l], one_all[l], two_all[l])
        for l in range(layers)
    ]

    own_pair = [lax.dynamic_index_in_dim(a, slot, 0, keepdims=False) for a in (tokens, cotangent)]
    own_pair = jnp.concatenate(own_pair, axis=1)
    pair = jnp.concatenate([own_pair, swap(own_pair)], axis=0)
    row = jnp.arange(rows)
    in_first = row < own_lengths[0]
    position = jnp.where(in_first, row, row - own_lengths[0])
    source = position + capacity * (jnp.where(in_first, 0, 1) != core)
    pick_rows = ((jnp.arange(2 * capacity)[None] == source[:, None]) & (row < SEQ)[:, None]).astype(BF)
    packed_pair = mm(pick_rows, pair).astype(BF)
    image = [packed_pair[:, :features], packed_pair[:, features:]]
    if order is not None:
        image = [mm(half, order) for half in image]
    stream = image[0].astype(F32)
    gradient = image[1].astype(F32) * row_mask

    weights = [tuple(first_qkv + gather_group(cut[0][1:3]) + gather_group(cut[0][3:]))]
    for l in range(1, layers):
        weights.append(tuple(gather_group(cut[l][:2]) + gather_group(cut[l][2:])))

    saved = []
    for l in range(layers):
        stream, items = forward_layer(stream, weights[l], vectors[l], key_valid)
        saved.append(items)

    place = jnp.arange(capacity)
    target = place + jnp.where(core == 0, 0, own_lengths[0])
    pick_back = (row[None] == target[:, None]) & ((place < own_lengths[core]) & live)[:, None]
    pick_back = pick_back.astype(BF)

    def give_back(values):
        values = values.astype(BF)
        if order is not None:
            values = mm_nt(values, order).astype(BF)
        return lax.all_gather(mm(pick_back, values).astype(BF), "tp", axis=0)[:slots]

    output = give_back(stream)
    names = ("down", "up", "out", "qkv")
    found = {}
    sums = [None] * layers
    mine = [None] * layers
    for l in reversed(range(layers)):

        def emit(name, delta, values):
            found[name] = gradient_rows(delta, values).reshape(n_tp, -1, features // n_fsdp)

        if l == layers - 2:
            gradient, output = lax.optimization_barrier((gradient, output))
        gradient, sums[l] = backward_layer(gradient, saved[l], weights[l], vectors[l], key_valid, emit)
        together = lambda some: jnp.concatenate([found[name] for name in some], axis=1)
        if l > 0:
            mine[l] = lax.psum_scatter(together(names), "tp", scatter_dimension=0, tiled=False)
        else:
            early = lax.psum_scatter(together(names[:2]), "tp", scatter_dimension=0, tiled=False)
            mine[l] = jnp.concatenate([early, scatter_line(together(names[2:]))], axis=0)
    input_grad = give_back(gradient)

    grads = {name: [] for name in names}
    heights = [2 * found[name].shape[1] // 2 for name in names]
    for l in range(layers):
        other = swap(mine[l])
        low = jnp.where(core == 0, mine[l], other)
        high = jnp.where(core == 0, other, mine[l])
        start = 0
        for name, height in zip(names, heights):
            grads[name].append((low[start : start + height], high[start : start + height]))
            start += height
    rows_joined = lambda name: jnp.stack([jnp.concatenate(p, axis=0) for p in grads[name]]).astype(F32)
    turned = lambda name: jnp.stack([jnp.concatenate([h.T for h in p], axis=1) for p in grads[name]]).astype(F32)
    depth = features // n_fsdp
    qkv_grad = jnp.stack(
        [
            jnp.concatenate([jnp.transpose(h.reshape(3, -1, depth), (2, 0, 1)) for h in p], axis=2)
            for p in grads["qkv"]
        ]
    ).astype(F32)

    def from_core(array, count):
        array = array.reshape(layers, count, n_tp, 1, -1)
        mask = (jnp.arange(2) == core)[:, None]
        return jnp.where(mask, array, 0.0).reshape(-1)

    first = (core == 0).astype(F32)
    member = lambda k: jnp.stack([sums[l][k] for l in range(layers)])
    by_feature = jnp.stack([member(k) for k in (2, 4, 5, 6)]).reshape(4 * layers, features) * first
    if order is not None:
        by_feature = lax.dot_general(
            by_feature, order.astype(F32), (((1,), (1,)), ((), ())), precision=lax.Precision.HIGHEST
        )
    joined = [
        from_core(jnp.stack([member(0), member(1)], axis=1), 2),
        from_core(member(3)[:, None], 1),
        by_feature.reshape(-1),
    ]
    summed = jnp.concatenate(joined).reshape(-1, 128)
    if square() and n_tp == 4:
        summed = summed + swap(summed)
        summed = summed + send_x(summed)
        summed = summed + send_y(summed)
        summed = summed + lax.ppermute(summed, "tp", [(0, 1), (1, 0), (2, 3), (3, 2)])
        summed = summed + lax.ppermute(summed, "tp", [(0, 2), (2, 0), (1, 3), (3, 1)])
    else:
        summed = lax.psum(summed, ("fsdp", "ctx", "tp"))
    summed = summed.reshape(-1)
    pick = lambda a, i, axis: lax.dynamic_index_in_dim(a, i, axis, keepdims=True)
    ends = (joined[0].size, joined[0].size + joined[1].size)
    qv_grad = pick(pick(summed[: ends[0]].reshape(layers, 2, n_tp, n_fsdp, -1), lane, 2), group, 3)[:, :, :, 0]
    up_grad = pick(pick(summed[ends[0] : ends[1]].reshape(layers, n_tp, n_fsdp, -1), lane, 1), group, 2)[:, :, 0]
    out_shift, down_shift, one, two = pick(summed[ends[1] :].reshape(4, layers, n_fsdp, -1), group, 2)[:, :, 0]
    return (
        output,
        input_grad,
        qkv_grad,
        qv_grad,
        rows_joined("out"),
        out_shift,
        turned("up"),
        up_grad,
        rows_joined("down"),
        down_shift,
        one,
        two,
    )


def solution(mesh):
    in_specs = (
        P("fsdp", "ctx", None),
        P("fsdp", None),
        P("fsdp"),
        P(None, "fsdp", None, "tp"),
        P(None, None, "tp", "fsdp"),
        P(None, "tp", "fsdp"),
        P(None, "fsdp"),
        P(None, "fsdp", "tp"),
        P(None, "tp", "fsdp"),
        P(None, "tp", "fsdp"),
        P(None, "fsdp"),
        P(None, "fsdp"),
        P(None, "fsdp"),
        P("fsdp", "ctx", None),
    )
    out_specs = (
        P("fsdp", "ctx", None),
        P("fsdp", "ctx", None),
        P(None, "fsdp", None, "tp"),
        P(None, None, "tp", "fsdp"),
        P(None, "tp", "fsdp"),
        P(None, "fsdp"),
        P(None, "fsdp", "tp"),
        P(None, "tp", "fsdp"),
        P(None, "tp", "fsdp"),
        P(None, "fsdp"),
        P(None, "fsdp"),
        P(None, "fsdp"),
    )
    return jax.shard_map(shards, mesh=mesh, in_specs=in_specs, out_specs=out_specs, check_vma=False)
```

```python
import jax
import jax.numpy as jnp
from jax import lax
from jax.experimental import pallas as pl
from jax.experimental.pallas import tpu as pltpu
from jax.sharding import PartitionSpec as P

HD = 64
SEQ = 577
BF = jnp.bfloat16
F32 = jnp.float32


def layer_norm(vectors, scaling):
    centre = vectors - jnp.mean(vectors, axis=-1, keepdims=True)
    spread = jnp.mean(centre * centre, axis=-1, keepdims=True)
    return centre * lax.rsqrt(spread + 1e-06) * scaling


def gelu_exact(values):
    return 0.5 * values * (1.0 + lax.erf(values * 0.7071067811865476))


X_PAIRS = [(0, 1), (1, 0), (2, 3), (3, 2)]
Y_PAIRS = [(0, 2), (2, 0), (1, 3), (3, 1)]
BLOCKS = ((0, 0), (0, 1), (1, 1), (2, 0), (1, 0), (3, 0), (3, 1), (2, 1))


def square():
    return lax.axis_size("fsdp") == 4


def order_matrix(features):
    if not square():
        return None
    half = features // 8
    group = lax.axis_index("fsdp")
    starts = jnp.stack([((group ^ other) * 2 + part) * half for other, part in BLOCKS])
    natural = (starts[:, None] + jnp.arange(half)[None]).reshape(-1)
    return (jnp.arange(features)[:, None] == natural[None]).astype(BF)


def send_x(values):
    return lax.ppermute(values, "fsdp", X_PAIRS)


def send_y(values):
    return lax.ppermute(values, "fsdp", Y_PAIRS)


def after(values, *earlier):
    return lax.optimization_barrier((values,) + earlier)[0]


def swap(values):
    return lax.ppermute(values, "ctx", [(0, 1), (1, 0)])


def both_cores(partial_sum):
    low = partial_sum.astype(BF)
    return low.astype(F32) + swap(low).astype(F32)


def gather_line(shard):
    count, lane = lax.axis_size("tp"), lax.axis_index("tp")
    up_pairs = [(j, j + 1) for j in range(count - 1)]
    down_pairs = [(j + 1, j) for j in range(count - 1)]
    lower, upper = [shard], [shard]
    for step in range(count - 1):
        lower.append(lax.ppermute(lower[-1], "tp", up_pairs[step:]))
        upper.append(lax.ppermute(upper[-1], "tp", down_pairs[: count - 1 - step]))
    placed = []
    for owner in range(count):
        piece = shard
        for away in range(1, count):
            piece = jnp.where(lane == owner + away, lower[away], piece)
            piece = jnp.where(lane == owner - away, upper[away], piece)
        placed.append(piece)
    return jnp.stack(placed)


def scatter_line(full):
    count, lane = lax.axis_size("tp"), lax.axis_index("tp")
    take = lambda k: lax.dynamic_index_in_dim(full, jnp.clip(k, 0, count - 1), 0, keepdims=False)
    rising = falling = None
    for step in range(count - 1):
        to_up, to_down = take(lane + count - 1 - step), take(lane - (count - 1 - step))
        if step:
            to_up, to_down = to_up + rising, to_down + falling
        rising = lax.ppermute(to_up, "tp", [(j, j + 1) for j in range(step + 1)])
        falling = lax.ppermute(to_down, "tp", [(j + 1, j) for j in range(count - 2 - step, count - 1)])
    return (take(lane).astype(F32) + rising.astype(F32) + falling.astype(F32)).astype(BF)


def gather_features(along, previous):
    if not square():
        return [lax.all_gather(along, "fsdp", axis=along.ndim - 1, tiled=True)], ()
    half = along.shape[-1] // 2
    along = after(along, *previous)
    from_x, from_y = send_x(along), send_y(along)
    far_a, far_b = send_y(from_x[..., :half]), send_x(from_y[..., half:])
    pieces = [along, from_x[..., half:], from_y[..., :half], from_x[..., :half], far_a, far_b, from_y[..., half:]]
    return pieces, (from_x, from_y)


def gather_group(along, heights, previous):
    count = lax.axis_size("tp")
    pieces, came = gather_features(along, previous)
    pieces = [piece.reshape(count, -1, piece.shape[-1]) for piece in pieces]
    result, start = [], 0
    for height in heights:
        cut = [piece[:, start : start + height].reshape(count * height, -1) for piece in pieces]
        result.append(jnp.concatenate(cut, axis=1))
        start += height
    return result, came


def gradient_start(delta, values):
    if not square():
        return lax.psum_scatter(mm_tn(delta, values).astype(BF), "fsdp", scatter_dimension=1, tiled=True)
    half = values.shape[1] // 8
    to_x = mm_tn(delta, values[:, 4 * half : 6 * half]).astype(BF)
    from_x = send_x(to_x)
    to_y = mm_tn(delta, values[:, 6 * half :]).astype(BF)
    from_y = send_y(to_y)
    return mm_tn(delta, values[:, : 4 * half]).astype(BF), from_x, from_y


def gradient_finish(begun, *earlier):
    if not square():
        return begun
    kept, from_x, from_y = begun
    half = from_x.shape[1] // 2
    if earlier:
        from_x, from_y = lax.optimization_barrier((from_x, from_y) + earlier)[:2]
    own_a, own_b, x_b, y_a = jnp.split(kept, 4, axis=1)
    last_a = send_y(y_a + from_x[:, half:])
    last_b = send_x(x_b + from_y[:, :half])
    add = lambda *terms: sum(term.astype(F32) for term in terms).astype(BF)
    return jnp.concatenate([add(own_a, from_x[:, :half], last_a), add(own_b, from_y[:, half:], last_b)], axis=1)


def mm(left, right):
    return jnp.dot(left, right, preferred_element_type=F32)


def mm_nt(left, right):
    return lax.dot_general(left, right, (((1,), (1,)), ((), ())), preferred_element_type=F32)


def mm_tn(left, right):
    return lax.dot_general(left, right, (((0,), (0,)), ((), ())), preferred_element_type=F32)


def head_scores(project_ref, tile, head):
    part = lambda k: project_ref[:, k * tile + head * HD : k * tile + (head + 1) * HD]
    queries, keys, values = part(0), part(1), part(2)
    scores = mm_nt(queries * BF(HD ** (-0.5)), keys)
    valid = lax.broadcasted_iota(jnp.int32, (1, scores.shape[1]), 1) < SEQ
    return queries, keys, values, jnp.where(valid, scores, -1000000000.0)


def attend_kernel(project_ref, mixed_ref, total_ref):
    tile = mixed_ref.shape[1]
    mixed, totals = [], []
    for head in range(tile // HD):
        values, scores = head_scores(project_ref, tile, head)[2:]
        highest = jnp.max(scores, axis=1, keepdims=True)
        exponent = jnp.exp(scores - highest)
        denominator = jnp.sum(exponent, axis=1, keepdims=True)
        mixed.append(mm(exponent.astype(BF), values) / denominator)
        totals.append(highest + jnp.log(denominator))
    mixed_ref[...] = jnp.concatenate(mixed, axis=1).astype(BF)
    total_ref[0] = jnp.concatenate(totals, axis=1)


def attend_back_kernel(project_ref, mixed_ref, total_ref, delta_ref, out_ref):
    tile = mixed_ref.shape[1]
    scale = HD ** (-0.5)
    parts = ([], [], [])
    for head in range(tile // HD):
        queries, keys, values, scores = head_scores(project_ref, tile, head)
        here = slice(head * HD, (head + 1) * HD)
        delta = delta_ref[:, here]
        probs = jnp.exp(scores - total_ref[0, :, head : head + 1])
        inner = jnp.sum(delta.astype(F32) * mixed_ref[:, here].astype(F32), axis=1, keepdims=True)
        delta_scores = (probs * (mm_nt(delta, values) - inner)).astype(BF)
        parts[0].append(mm(delta_scores, keys) * scale)
        parts[1].append(mm_tn(delta_scores, queries) * scale)
        parts[2].append(mm_tn(probs.astype(BF), delta))
    out_ref[...] = jnp.concatenate(parts[0] + parts[1] + parts[2], axis=1).astype(BF)


def attention_specs(rows, tile):
    wide = pl.BlockSpec((rows, 3 * tile), lambda t: (0, t))
    narrow = pl.BlockSpec((rows, tile), lambda t: (0, t))
    totals = pl.BlockSpec((1, rows, tile // HD), lambda t: (t, 0, 0))
    return wide, narrow, totals


def attend(project, tile):
    rows, count = project.shape[0], project.shape[1] // (3 * tile)
    wide, narrow, totals = attention_specs(rows, tile)
    work = rows * rows * tile * count
    return pl.pallas_call(
        attend_kernel,
        grid=(count,),
        in_specs=[wide],
        out_specs=[narrow, totals],
        out_shape=[
            jax.ShapeDtypeStruct((rows, tile * count), BF),
            jax.ShapeDtypeStruct((count, rows, tile // HD), F32),
        ],
        compiler_params=pltpu.CompilerParams(vmem_limit_bytes=32 * 1024 * 1024),
        cost_estimate=pl.CostEstimate(flops=16 * work, bytes_accessed=8 * project.size // 3, transcendentals=work // HD),
    )(project)


def attend_back(project, mixed, totals, delta, tile):
    rows, count = project.shape[0], project.shape[1] // (3 * tile)
    wide, narrow, per_row = attention_specs(rows, tile)
    work = rows * rows * tile * count
    return pl.pallas_call(
        attend_back_kernel,
        grid=(count,),
        in_specs=[wide, narrow, per_row, narrow],
        out_specs=wide,
        out_shape=jax.ShapeDtypeStruct(project.shape, BF),
        compiler_params=pltpu.CompilerParams(vmem_limit_bytes=32 * 1024 * 1024),
        cost_estimate=pl.CostEstimate(flops=40 * work, bytes_accessed=5 * project.size, transcendentals=work // HD),
    )(project, mixed, totals, delta)


def forward_layer(stream, weights, vectors, gates):
    qkv, out, up, down = weights
    qkv_shift, out_shift, up_shift, down_shift, gain_first, gain_second = vectors
    normed = layer_norm(stream, gain_first).astype(BF)
    project = (mm_nt(normed, qkv) + qkv_shift).astype(BF)
    tile = project.shape[1] // (3 * lax.axis_size("tp"))
    mixed, totals = attend(after(project, *gates[0]), tile)
    mixed = after(mixed, *gates[1])
    middle = stream + both_cores(mm(mixed, out)) + out_shift
    normed_b = layer_norm(middle, gain_second).astype(BF)
    hidden = mm_nt(normed_b, up) + up_shift
    active = gelu_exact(hidden).astype(BF)
    following = middle + both_cores(mm(active, down)) + down_shift
    return following, (stream, normed, project, totals, mixed, middle, normed_b, hidden, active)


def backward_layer(gradient, saved, weights, vectors, emit, gate):
    qkv, out, up, down = weights
    gain_first, gain_second = vectors[4:]
    stream, normed, project, totals, mixed, middle, normed_b, hidden, active = saved
    total = lambda array: jnp.sum(array.astype(F32), axis=0)
    grad_low = gradient.astype(BF)
    emit("down", active, grad_low)
    delta_hidden = jax.vjp(gelu_exact, hidden)[1](mm_nt(grad_low, down))[0].astype(BF)
    delta_hidden = gate("hidden", delta_hidden)
    emit("up", delta_hidden, normed_b)
    delta_normed_b = both_cores(mm(delta_hidden, up))
    back_middle, delta_gain_second = jax.vjp(layer_norm, middle, gain_second)[1](delta_normed_b)
    grad_middle = gradient + back_middle
    grad_attend = grad_middle.astype(BF)
    grad_attend = gate("attend", grad_attend)
    emit("out", mixed, grad_attend)
    delta_mixed = mm_nt(grad_attend, out).astype(BF)
    tile = mixed.shape[1] // lax.axis_size("tp")
    delta_project = attend_back(project, mixed, totals, delta_mixed, tile)
    delta_project = gate("project", delta_project)
    emit("qkv", delta_project, normed)
    delta_normed = both_cores(mm(delta_project, qkv))
    back_stream, delta_gain_first = jax.vjp(layer_norm, stream, gain_first)[1](delta_normed)
    sums = (
        total(delta_project),
        total(grad_attend),
        total(delta_hidden),
        total(grad_low),
        delta_gain_first,
        delta_gain_second,
    )
    return grad_middle + back_stream, sums


def shards(
    tokens,
    lengths,
    image_count,
    qkv_weight,
    qv_bias,
    out_weight,
    out_bias,
    up_weight,
    up_bias,
    down_weight,
    down_bias,
    gain_one,
    gain_two,
    cotangent,
):
    slots, capacity, features = tokens.shape
    layers = qkv_weight.shape[0]
    n_fsdp, n_tp = lax.axis_size("fsdp"), lax.axis_size("tp")
    assert lax.axis_size("ctx") == 2 and slots <= n_tp
    group, core, lane = lax.axis_index("fsdp"), lax.axis_index("ctx"), lax.axis_index("tp")
    rows = -(-SEQ // 16) * 16
    slot = jnp.minimum(lane, slots - 1)
    own_lengths = lax.dynamic_index_in_dim(lengths, slot, 0, keepdims=False)
    live = lane < jnp.minimum(image_count[0], slots)
    row_mask = ((jnp.arange(rows) < SEQ) & live).astype(F32)[:, None]
    halves = lambda array, axis: lax.dynamic_index_in_dim(
        array.reshape(array.shape[:axis] + (2, -1) + array.shape[axis + 1 :]), core, axis, keepdims=False
    )

    cut = []
    for l in range(layers):
        qkv = jnp.transpose(halves(qkv_weight[l], 2), (1, 2, 0)).reshape(-1, qkv_weight.shape[1])
        cut.append((qkv, halves(out_weight[l], 0), halves(up_weight[l], 1).T, halves(down_weight[l], 0)))
    heights = [piece.shape[0] for piece in cut[0]]
    joined = lambda l, members: jnp.concatenate([cut[l][k] for k in members], axis=0)
    groups = [[(0,), (1, 2), (3,)]] + [[(0, 1), (2,), (3,)]] * (layers - 1)
    stages, along = [], ()
    for l in range(layers):
        for members in groups[l]:
            shard = after(joined(l, members), *along)
            if l == 0 and members == (0,):
                along = (gather_line(shard).reshape(-1, shard.shape[1]),)
            else:
                along = (lax.all_gather(shard, "tp", axis=0, tiled=True),)
            stages.append((l, members, along[0]))
    first_along = stages[0][2]

    pieces = (qv_bias, up_bias, out_bias, down_bias, gain_one, gain_two)
    packed = jnp.concatenate([piece.reshape(1, -1) for piece in pieces], axis=1)
    if square():
        near_x, near_y = send_x(packed), send_y(packed)
        found = jnp.concatenate([packed, near_x, near_y, send_y(near_x)])
        natural = [lax.dynamic_index_in_dim(found, group ^ k, 0, keepdims=False) for k in range(4)]
        spread = jnp.stack(natural)
    else:
        spread = lax.all_gather(packed[0], "fsdp", axis=0)
    order = order_matrix(features)
    split = qv_bias.size + up_bias.size
    across = gather_line(after(spread[:, :split], first_along))

    def by_core(array, count):
        array = array.reshape(n_tp, n_fsdp, layers, count, -1)
        array = jnp.transpose(array, (2, 3, 0, 1, 4)).reshape(layers, count, n_tp, 2, -1)
        return lax.dynamic_index_in_dim(array, core, 3, keepdims=False).reshape(layers, count, -1)

    qv_all = by_core(across[:, :, : qv_bias.size], 2)
    up_all = by_core(across[:, :, qv_bias.size :], 1)
    by_feature = jnp.transpose(spread[:, split:].reshape(n_fsdp, 4, layers, -1), (1, 2, 0, 3)).reshape(4 * layers, features)
    if order is not None:
        by_feature = mm(by_feature, order)
    by_feature = by_feature.astype(F32).reshape(4, layers, features)
    out_all, down_all, one_all, two_all = by_feature[0], by_feature[1], by_feature[2], by_feature[3]
    q_part, v_part = [qv_all[:, k].reshape(layers, n_tp, -1) for k in range(2)]
    qkv_all = jnp.concatenate([q_part, jnp.zeros_like(q_part), v_part], axis=2).reshape(layers, -1).astype(F32)
    vectors = [
        (qkv_all[l], out_all[l], up_all[l, 0], down_all[l], one_all[l], two_all[l])
        for l in range(layers)
    ]

    own_pair = [lax.dynamic_index_in_dim(a, slot, 0, keepdims=False) for a in (tokens, cotangent)]
    own_pair = jnp.concatenate(own_pair, axis=1)
    pair = jnp.concatenate([own_pair, swap(own_pair)], axis=0)
    row = jnp.arange(rows)
    in_first = row < own_lengths[0]
    position = jnp.where(in_first, row, row - own_lengths[0])
    source = position + capacity * (jnp.where(in_first, 0, 1) != core)
    pick_rows = ((jnp.arange(2 * capacity)[None] == source[:, None]) & (row < SEQ)[:, None]).astype(BF)
    packed_pair = mm(pick_rows, pair).astype(BF)
    image = [packed_pair[:, :features], packed_pair[:, features:]]
    if order is not None:
        image = [mm(half, order) for half in image]
    stream = image[0].astype(F32)
    gradient = image[1].astype(F32) * row_mask

    weights = [[] for l in range(layers)]
    came, arrivals = (), []
    for l, members, along in stages:
        more, came = gather_group(along, [heights[k] for k in members], came)
        weights[l] += more
        arrivals.append(came)

    saved = []
    for l in range(layers):
        stream, items = forward_layer(stream, weights[l], vectors[l], arrivals[3 * l + 1 : 3 * l + 3])
        saved.append(items)

    place = jnp.arange(capacity)
    target = place + jnp.where(core == 0, 0, own_lengths[0])
    pick_back = (row[None] == target[:, None]) & ((place < own_lengths[core]) & live)[:, None]
    pick_back = pick_back.astype(BF)

    def give_back(values):
        values = values.astype(BF)
        if order is not None:
            values = mm_nt(values, order).astype(BF)
        return mm(pick_back, values).astype(BF)

    def to_all(values):
        return lax.all_gather(values, "tp", axis=0)[:slots]

    output = give_back(stream)
    gradient, output = lax.optimization_barrier((gradient, output))
    output = to_all(output)
    names = ("down", "up", "out", "qkv")
    begun, found = {}, {}
    sums = [None] * layers
    mine = [None] * layers

    def reduced(layer, some):
        joined = [found[layer, name].reshape(n_tp, -1, features // n_fsdp) for name in some]
        return jnp.concatenate(joined, axis=1)

    for l in reversed(range(layers)):

        def emit(name, delta, values, l=l):
            begun[l, name] = gradient_start(delta, values)

        def first(name, layer):
            found[layer, name] = gradient_finish(begun[layer, name])
            return begun[layer, name][1:] if square() else ()

        def gate(point, value, l=l):
            held = ()
            if point == "hidden" and l < layers - 1:
                held = first("out", l + 1) + (found[l + 1, "down"],)
            if point == "attend":
                held = first("down", l)
                if l < layers - 1:
                    held += first("qkv", l + 1) + (found[l + 1, "up"], found[l + 1, "out"])
            if point == "project":
                held = first("up", l)
                if l < layers - 1:
                    mine[l + 1] = lax.psum_scatter(reduced(l + 1, names), "tp", scatter_dimension=0, tiled=False)
                    held += (output, found[l, "down"])
            return after(value, *held)

        gradient, sums[l] = backward_layer(gradient, saved[l], weights[l], vectors[l], emit, gate)
    found[0, "out"] = gradient_finish(begun[0, "out"])
    early = lax.psum_scatter(reduced(0, names[:3]), "tp", scatter_dimension=0, tiled=False)
    found[0, "qkv"] = gradient_finish(begun[0, "qkv"])
    mine[0] = jnp.concatenate([early, scatter_line(reduced(0, names[3:]))], axis=0)
    input_grad = to_all(give_back(gradient))

    grads = {name: [] for name in names}
    heights = [found[0, name].shape[0] // n_tp for name in names]
    for l in range(layers):
        other = swap(mine[l])
        low = jnp.where(core == 0, mine[l], other)
        high = jnp.where(core == 0, other, mine[l])
        start = 0
        for name, height in zip(names, heights):
            grads[name].append((low[start : start + height], high[start : start + height]))
            start += height
    rows_joined = lambda name: jnp.stack([jnp.concatenate(p, axis=0) for p in grads[name]]).astype(F32)
    turned = lambda name: jnp.stack([jnp.concatenate([h.T for h in p], axis=1) for p in grads[name]]).astype(F32)
    depth = features // n_fsdp
    qkv_grad = jnp.stack(
        [
            jnp.concatenate([jnp.transpose(h.reshape(3, -1, depth), (2, 0, 1)) for h in p], axis=2)
            for p in grads["qkv"]
        ]
    ).astype(F32)

    def from_core(array, count):
        array = array.reshape(layers, count, n_tp, 1, -1)
        mask = (jnp.arange(2) == core)[:, None]
        return jnp.where(mask, array, 0.0).reshape(-1)

    first = (core == 0).astype(F32)
    member = lambda k: jnp.stack([sums[l][k] for l in range(layers)])
    by_feature = jnp.stack([member(k) for k in (1, 3, 4, 5)]).reshape(4 * layers, features) * first
    if order is not None:
        by_feature = lax.dot_general(
            by_feature, order.astype(F32), (((1,), (1,)), ((), ())), precision=lax.Precision.HIGHEST
        )
    joined = [
        from_core(jnp.swapaxes(member(0).reshape(layers, n_tp, 3, -1)[:, :, ::2], 1, 2), 2),
        from_core(member(2)[:, None], 1),
        by_feature.reshape(-1),
    ]
    summed = jnp.concatenate(joined).reshape(-1, 128)
    if square() and n_tp == 4:
        summed = summed + swap(summed)
        summed = summed + send_x(summed)
        summed = summed + send_y(summed)
        summed = summed + lax.ppermute(summed, "tp", [(0, 1), (1, 0), (2, 3), (3, 2)])
        summed = summed + lax.ppermute(summed, "tp", [(0, 2), (2, 0), (1, 3), (3, 1)])
    else:
        summed = lax.psum(summed, ("fsdp", "ctx", "tp"))
    summed = summed.reshape(-1)
    pick = lambda a, i, axis: lax.dynamic_index_in_dim(a, i, axis, keepdims=True)
    ends = (joined[0].size, joined[0].size + joined[1].size)
    qv_grad = pick(pick(summed[: ends[0]].reshape(layers, 2, n_tp, n_fsdp, -1), lane, 2), group, 3)[:, :, :, 0]
    up_grad = pick(pick(summed[ends[0] : ends[1]].reshape(layers, n_tp, n_fsdp, -1), lane, 1), group, 2)[:, :, 0]
    out_shift, down_shift, one, two = pick(summed[ends[1] :].reshape(4, layers, n_fsdp, -1), group, 2)[:, :, 0]
    return (
        output,
        input_grad,
        qkv_grad,
        qv_grad,
        rows_joined("out"),
        out_shift,
        turned("up"),
        up_grad,
        rows_joined("down"),
        down_shift,
        one,
        two,
    )


def solution(mesh):
    in_specs = (
        P("fsdp", "ctx", None),
        P("fsdp", None),
        P("fsdp"),
        P(None, "fsdp", None, "tp"),
        P(None, None, "tp", "fsdp"),
        P(None, "tp", "fsdp"),
        P(None, "fsdp"),
        P(None, "fsdp", "tp"),
        P(None, "tp", "fsdp"),
        P(None, "tp", "fsdp"),
        P(None, "fsdp"),
        P(None, "fsdp"),
        P(None, "fsdp"),
        P("fsdp", "ctx", None),
    )
    out_specs = (
        P("fsdp", "ctx", None),
        P("fsdp", "ctx", None),
        P(None, "fsdp", None, "tp"),
        P(None, None, "tp", "fsdp"),
        P(None, "tp", "fsdp"),
        P(None, "fsdp"),
        P(None, "fsdp", "tp"),
        P(None, "tp", "fsdp"),
        P(None, "tp", "fsdp"),
        P(None, "fsdp"),
        P(None, "fsdp"),
        P(None, "fsdp"),
    )
    return jax.shard_map(shards, mesh=mesh, in_specs=in_specs, out_specs=out_specs, check_vma=False)
```

```python
import jax
import jax.numpy as jnp
from jax import lax
from jax.experimental import pallas as pl
from jax.experimental.pallas import tpu as pltpu
from jax.sharding import PartitionSpec as P

HD = 64
SEQ = 577
BF = jnp.bfloat16
F32 = jnp.float32


def layer_norm(vectors, scaling):
    centre = vectors - jnp.mean(vectors, axis=-1, keepdims=True)
    spread = jnp.mean(centre * centre, axis=-1, keepdims=True)
    return centre * lax.rsqrt(spread + 1e-06) * scaling


def gelu_exact(values):
    return 0.5 * values * (1.0 + lax.erf(values * 0.7071067811865476))


X_PAIRS = [(0, 1), (1, 0), (2, 3), (3, 2)]
Y_PAIRS = [(0, 2), (2, 0), (1, 3), (3, 1)]
BLOCKS = ((0, 0), (0, 1), (1, 1), (2, 0), (1, 0), (3, 0), (3, 1), (2, 1))


def square():
    return lax.axis_size("fsdp") == 4


def order_matrix(features):
    if not square():
        return None
    half = features // 8
    group = lax.axis_index("fsdp")
    starts = jnp.stack([((group ^ other) * 2 + part) * half for other, part in BLOCKS])
    natural = (starts[:, None] + jnp.arange(half)[None]).reshape(-1)
    return (jnp.arange(features)[:, None] == natural[None]).astype(BF)


def send_x(values):
    return lax.ppermute(values, "fsdp", X_PAIRS)


def send_y(values):
    return lax.ppermute(values, "fsdp", Y_PAIRS)


def after(values, *earlier):
    return lax.optimization_barrier((values,) + earlier)[0]


def swap(values):
    return lax.ppermute(values, "ctx", [(0, 1), (1, 0)])


def both_cores(partial_sum):
    low = partial_sum.astype(BF)
    return low.astype(F32) + swap(low).astype(F32)


def tp_bits():
    count = lax.axis_size("tp")
    bits = [1 << k for k in reversed(range(count.bit_length() - 1))]
    assert 1 << len(bits) == count
    return [(bit, axis) for axis, bit in enumerate(bits)]


def tp_partner(values, bit):
    return lax.ppermute(values, "tp", [(j, j ^ bit) for j in range(lax.axis_size("tp"))])


def gather_pairs(shard):
    lane, held = lax.axis_index("tp"), shard
    for bit, axis in tp_bits():
        other = tp_partner(held, bit)
        upper = (lane & bit) != 0
        held = jnp.stack([jnp.where(upper, other, held), jnp.where(upper, held, other)], axis=axis)
    return held.reshape((-1,) + shard.shape)


def scatter_pairs(full):
    lane, bits = lax.axis_index("tp"), tp_bits()
    held = full.reshape((2,) * len(bits) + full.shape[1:])
    for bit, axis in reversed(bits):
        mine = jnp.where((lane & bit) != 0, 1, 0)
        take = lambda k: lax.dynamic_index_in_dim(held, k, axis, keepdims=False)
        other = tp_partner(take(1 - mine), bit)
        held = (take(mine).astype(F32) + other.astype(F32)).astype(BF)
    return held


def gather_features(along, previous):
    if not square():
        return [lax.all_gather(along, "fsdp", axis=along.ndim - 1, tiled=True)], ()
    half = along.shape[-1] // 2
    along = after(along, *previous)
    from_x, from_y = send_x(along), send_y(along)
    far_a, far_b = send_y(from_x[..., :half]), send_x(from_y[..., half:])
    pieces = [along, from_x[..., half:], from_y[..., :half], from_x[..., :half], far_a, far_b, from_y[..., half:]]
    return pieces, (from_x, from_y)


def gather_group(along, heights, previous):
    count = lax.axis_size("tp")
    pieces, came = gather_features(along, previous)
    pieces = [piece.reshape(count, -1, piece.shape[-1]) for piece in pieces]
    result, start = [], 0
    for height in heights:
        cut = [piece[:, start : start + height].reshape(count * height, -1) for piece in pieces]
        result.append(jnp.concatenate(cut, axis=1))
        start += height
    return result, came


def gradient_start(delta, values):
    if not square():
        return lax.psum_scatter(mm_tn(delta, values).astype(BF), "fsdp", scatter_dimension=1, tiled=True)
    half = values.shape[1] // 8
    to_x = mm_tn(delta, values[:, 4 * half : 6 * half]).astype(BF)
    from_x = send_x(to_x)
    to_y = mm_tn(delta, values[:, 6 * half :]).astype(BF)
    from_y = send_y(to_y)
    return mm_tn(delta, values[:, : 4 * half]).astype(BF), from_x, from_y


def gradient_second(begun, marker):
    if not square():
        return begun
    kept, from_x, from_y = begun
    half = from_x.shape[1] // 2
    from_x, from_y = lax.optimization_barrier((from_x, from_y, marker))[:2]
    own_a, own_b, x_b, y_a = jnp.split(kept, 4, axis=1)
    last_a = send_y(y_a + from_x[:, half:])
    last_b = send_x(x_b + from_y[:, :half])
    return (own_a, from_x[:, :half], last_a), (own_b, from_y[:, half:], last_b)


def gradient_finish(terms, marker):
    if not square():
        return terms
    last_a, last_b = lax.optimization_barrier((terms[0][2], terms[1][2], marker))[:2]
    add = lambda own, near, last: (own.astype(F32) + near.astype(F32) + last.astype(F32)).astype(BF)
    return jnp.concatenate([add(*terms[0][:2], last_a), add(*terms[1][:2], last_b)], axis=1)


def mm(left, right):
    return jnp.dot(left, right, preferred_element_type=F32)


def mm_nt(left, right):
    return lax.dot_general(left, right, (((1,), (1,)), ((), ())), preferred_element_type=F32)


def mm_tn(left, right):
    return lax.dot_general(left, right, (((0,), (0,)), ((), ())), preferred_element_type=F32)


def head_scores(project_ref, tile, head):
    part = lambda k: project_ref[:, k * tile + head * HD : k * tile + (head + 1) * HD]
    queries, keys, values = part(0), part(1), part(2)
    scores = mm_nt(queries * BF(HD ** (-0.5)), keys)
    valid = lax.broadcasted_iota(jnp.int32, (1, scores.shape[1]), 1) < SEQ
    return queries, keys, values, jnp.where(valid, scores, -1000000000.0)


def attend_kernel(project_ref, mixed_ref, total_ref):
    tile = mixed_ref.shape[1]
    mixed, totals = [], []
    for head in range(tile // HD):
        values, scores = head_scores(project_ref, tile, head)[2:]
        highest = jnp.max(scores, axis=1, keepdims=True)
        exponent = jnp.exp(scores - highest)
        denominator = jnp.sum(exponent, axis=1, keepdims=True)
        mixed.append(mm(exponent.astype(BF), values) / denominator)
        totals.append(highest + jnp.log(denominator))
    mixed_ref[...] = jnp.concatenate(mixed, axis=1).astype(BF)
    total_ref[0] = jnp.concatenate(totals, axis=1)


def attend_back_kernel(project_ref, mixed_ref, total_ref, delta_ref, out_ref):
    tile = mixed_ref.shape[1]
    scale = HD ** (-0.5)
    parts = ([], [], [])
    for head in range(tile // HD):
        queries, keys, values, scores = head_scores(project_ref, tile, head)
        here = slice(head * HD, (head + 1) * HD)
        delta = delta_ref[:, here]
        probs = jnp.exp(scores - total_ref[0, :, head : head + 1])
        inner = jnp.sum(delta.astype(F32) * mixed_ref[:, here].astype(F32), axis=1, keepdims=True)
        delta_scores = (probs * (mm_nt(delta, values) - inner)).astype(BF)
        parts[0].append(mm(delta_scores, keys) * scale)
        parts[1].append(mm_tn(delta_scores, queries) * scale)
        parts[2].append(mm_tn(probs.astype(BF), delta))
    out_ref[...] = jnp.concatenate(parts[0] + parts[1] + parts[2], axis=1).astype(BF)


def attention_specs(rows, tile):
    wide = pl.BlockSpec((rows, 3 * tile), lambda t: (0, t))
    narrow = pl.BlockSpec((rows, tile), lambda t: (0, t))
    totals = pl.BlockSpec((1, rows, tile // HD), lambda t: (t, 0, 0))
    return wide, narrow, totals


def attend(project, tile):
    rows, count = project.shape[0], project.shape[1] // (3 * tile)
    wide, narrow, totals = attention_specs(rows, tile)
    work = rows * rows * tile * count
    return pl.pallas_call(
        attend_kernel,
        grid=(count,),
        in_specs=[wide],
        out_specs=[narrow, totals],
        out_shape=[
            jax.ShapeDtypeStruct((rows, tile * count), BF),
            jax.ShapeDtypeStruct((count, rows, tile // HD), F32),
        ],
        compiler_params=pltpu.CompilerParams(vmem_limit_bytes=32 * 1024 * 1024),
        cost_estimate=pl.CostEstimate(flops=16 * work, bytes_accessed=8 * project.size // 3, transcendentals=work // HD),
    )(project)


def attend_back(project, mixed, totals, delta, tile):
    rows, count = project.shape[0], project.shape[1] // (3 * tile)
    wide, narrow, per_row = attention_specs(rows, tile)
    work = rows * rows * tile * count
    return pl.pallas_call(
        attend_back_kernel,
        grid=(count,),
        in_specs=[wide, narrow, per_row, narrow],
        out_specs=wide,
        out_shape=jax.ShapeDtypeStruct(project.shape, BF),
        compiler_params=pltpu.CompilerParams(vmem_limit_bytes=32 * 1024 * 1024),
        cost_estimate=pl.CostEstimate(flops=40 * work, bytes_accessed=5 * project.size, transcendentals=work // HD),
    )(project, mixed, totals, delta)


def forward_layer(stream, weights, vectors, gates):
    qkv, out, up, down = weights
    qkv_shift, out_shift, up_shift, down_shift, gain_first, gain_second = vectors
    normed = layer_norm(stream, gain_first).astype(BF)
    project = (mm_nt(normed, qkv) + qkv_shift).astype(BF)
    tile = project.shape[1] // (3 * lax.axis_size("tp"))
    mixed, totals = attend(after(project, *gates[0]), tile)
    mixed = after(mixed, *gates[1])
    middle = stream + both_cores(mm(mixed, out)) + out_shift
    normed_b = layer_norm(middle, gain_second).astype(BF)
    hidden = mm_nt(normed_b, up) + up_shift
    active = gelu_exact(hidden).astype(BF)
    following = middle + both_cores(mm(active, down)) + down_shift
    return following, (stream, normed, project, totals, mixed, middle, normed_b, hidden, active)


def backward_layer(gradient, saved, weights, vectors, emit, gate):
    qkv, out, up, down = weights
    gain_first, gain_second = vectors[4:]
    stream, normed, project, totals, mixed, middle, normed_b, hidden, active = saved
    total = lambda array: jnp.sum(array.astype(F32), axis=0)
    grad_low = gradient.astype(BF)
    emit("down", active, grad_low)
    delta_hidden = jax.vjp(gelu_exact, hidden)[1](mm_nt(grad_low, down))[0].astype(BF)
    delta_hidden = gate("hidden", delta_hidden)
    emit("up", delta_hidden, normed_b)
    delta_normed_b = both_cores(mm(delta_hidden, up))
    back_middle, delta_gain_second = jax.vjp(layer_norm, middle, gain_second)[1](delta_normed_b)
    grad_middle = gradient + back_middle
    grad_attend = grad_middle.astype(BF)
    grad_attend = gate("attend", grad_attend)
    emit("out", mixed, grad_attend)
    delta_mixed = gate("mixed", mm_nt(grad_attend, out).astype(BF))
    tile = mixed.shape[1] // lax.axis_size("tp")
    delta_project = attend_back(project, mixed, totals, delta_mixed, tile)
    delta_project = gate("project", delta_project)
    low = mm(delta_project, qkv).astype(BF)
    emit("qkv", after(delta_project, low), normed)
    delta_normed = gate("normed", low.astype(F32) + swap(low).astype(F32))
    back_stream, delta_gain_first = jax.vjp(layer_norm, stream, gain_first)[1](delta_normed)
    sums = (
        total(delta_project),
        total(grad_attend),
        total(delta_hidden),
        total(grad_low),
        delta_gain_first,
        delta_gain_second,
    )
    return grad_middle + back_stream, sums


def shards(
    tokens,
    lengths,
    image_count,
    qkv_weight,
    qv_bias,
    out_weight,
    out_bias,
    up_weight,
    up_bias,
    down_weight,
    down_bias,
    gain_one,
    gain_two,
    cotangent,
):
    slots, capacity, features = tokens.shape
    layers = qkv_weight.shape[0]
    n_fsdp, n_tp = lax.axis_size("fsdp"), lax.axis_size("tp")
    assert lax.axis_size("ctx") == 2 and slots <= n_tp
    group, core, lane = lax.axis_index("fsdp"), lax.axis_index("ctx"), lax.axis_index("tp")
    rows = -(-SEQ // 16) * 16
    slot = jnp.minimum(lane, slots - 1)
    own_lengths = lax.dynamic_index_in_dim(lengths, slot, 0, keepdims=False)
    live = lane < jnp.minimum(image_count[0], slots)
    row_mask = ((jnp.arange(rows) < SEQ) & live).astype(F32)[:, None]
    halves = lambda array, axis: lax.dynamic_index_in_dim(
        array.reshape(array.shape[:axis] + (2, -1) + array.shape[axis + 1 :]), core, axis, keepdims=False
    )

    cut = []
    for l in range(layers):
        qkv = jnp.transpose(halves(qkv_weight[l], 2), (1, 2, 0)).reshape(-1, qkv_weight.shape[1])
        cut.append((qkv, halves(out_weight[l], 0), halves(up_weight[l], 1).T, halves(down_weight[l], 0)))
    heights = [piece.shape[0] for piece in cut[0]]
    joined = lambda l, members: jnp.concatenate([cut[l][k] for k in members], axis=0)
    rows_of = lambda gathered, start, stop: gathered.reshape(n_tp, -1, gathered.shape[-1])[:, start:stop]
    first_along = gather_pairs(joined(0, (0,)))
    second_along = gather_pairs(after(joined(0, (1, 2)), first_along))
    stages = [(0, (0,), first_along), (0, (1, 2), second_along)]
    for l, members in [(0, (3,))] + [(l, some) for l in range(1, layers) for some in ((0, 1), (2, 3))]:
        gathered = lax.all_gather(after(joined(l, members), first_along), "tp", axis=0, tiled=True)
        first_along = gathered
        if members == (2, 3):
            stages.append((l, (2,), rows_of(gathered, 0, heights[2])))
            stages.append((l, (3,), rows_of(gathered, heights[2], None)))
        else:
            stages.append((l, members, gathered))
    stages = [(l, members, along.reshape(-1, along.shape[-1])) for l, members, along in stages]
    first_along = stages[0][2]

    pieces = (qv_bias, up_bias, out_bias, down_bias, gain_one, gain_two)
    packed = jnp.concatenate([piece.reshape(1, -1) for piece in pieces], axis=1)
    if square():
        near_x, near_y = send_x(packed), send_y(packed)
        found = jnp.concatenate([packed, near_x, near_y, send_y(near_x)])
        natural = [lax.dynamic_index_in_dim(found, group ^ k, 0, keepdims=False) for k in range(4)]
        spread = jnp.stack(natural)
    else:
        spread = lax.all_gather(packed[0], "fsdp", axis=0)
    order = order_matrix(features)
    split = qv_bias.size + up_bias.size
    across = gather_pairs(after(spread[:, :split], first_along))

    def by_core(array, count):
        array = array.reshape(n_tp, n_fsdp, layers, count, -1)
        array = jnp.transpose(array, (2, 3, 0, 1, 4)).reshape(layers, count, n_tp, 2, -1)
        return lax.dynamic_index_in_dim(array, core, 3, keepdims=False).reshape(layers, count, -1)

    qv_all = by_core(across[:, :, : qv_bias.size], 2)
    up_all = by_core(across[:, :, qv_bias.size :], 1)
    by_feature = jnp.transpose(spread[:, split:].reshape(n_fsdp, 4, layers, -1), (1, 2, 0, 3)).reshape(4 * layers, features)
    if order is not None:
        by_feature = mm(by_feature, order)
    by_feature = by_feature.astype(F32).reshape(4, layers, features)
    out_all, down_all, one_all, two_all = by_feature[0], by_feature[1], by_feature[2], by_feature[3]
    q_part, v_part = [qv_all[:, k].reshape(layers, n_tp, -1) for k in range(2)]
    qkv_all = jnp.concatenate([q_part, jnp.zeros_like(q_part), v_part], axis=2).reshape(layers, -1).astype(F32)
    vectors = [
        (qkv_all[l], out_all[l], up_all[l, 0], down_all[l], one_all[l], two_all[l])
        for l in range(layers)
    ]

    own_pair = [lax.dynamic_index_in_dim(a, slot, 0, keepdims=False) for a in (tokens, cotangent)]
    own_pair = jnp.concatenate(own_pair, axis=1)
    pair = jnp.concatenate([own_pair, swap(own_pair)], axis=0)
    row = jnp.arange(rows)
    in_first = row < own_lengths[0]
    position = jnp.where(in_first, row, row - own_lengths[0])
    source = position + capacity * (jnp.where(in_first, 0, 1) != core)
    pick_rows = ((jnp.arange(2 * capacity)[None] == source[:, None]) & (row < SEQ)[:, None]).astype(BF)
    packed_pair = mm(pick_rows, pair).astype(BF)
    image = [packed_pair[:, :features], packed_pair[:, features:]]
    if order is not None:
        image = [mm(half, order) for half in image]
    stream = image[0].astype(F32)
    gradient = image[1].astype(F32) * row_mask

    weights = [[] for l in range(layers)]
    came, arrivals = (), []
    for l, members, along in stages:
        more, came = gather_group(along, [heights[k] for k in members], came)
        weights[l] += more
        arrivals.append(came)

    saved = []
    for l in range(layers):
        stream, items = forward_layer(stream, weights[l], vectors[l], arrivals[3 * l + 1 : 3 * l + 3])
        saved.append(items)

    place = jnp.arange(capacity)
    target = place + jnp.where(core == 0, 0, own_lengths[0])
    pick_back = (row[None] == target[:, None]) & ((place < own_lengths[core]) & live)[:, None]
    pick_back = pick_back.astype(BF)

    def give_back(values):
        values = values.astype(BF)
        if order is not None:
            values = mm_nt(values, order).astype(BF)
        return mm(pick_back, values).astype(BF)

    def to_all(values):
        return lax.all_gather(values, "tp", axis=0)[:slots]

    output = give_back(stream)
    gradient, output = lax.optimization_barrier((gradient, output))
    output = to_all(output)
    names = ("down", "up", "out", "qkv")
    begun, found = {}, {}
    sums = [None] * layers

    further, along = {}, {}

    def second(layer, some, marker):
        held = ()
        for name in some:
            further[layer, name] = gradient_second(begun[layer, name], marker)
            held += begun[layer, name][1:] if square() else ()
        return held

    def finish(layer, some, marker):
        for name in some:
            found[layer, name] = gradient_finish(further[layer, name], marker)

    def along_tp(layer, some):
        return lax.psum_scatter(reduced(layer, some), "tp", scatter_dimension=0, tiled=False)

    def reduced(layer, some):
        joined = [found[layer, name].reshape(n_tp, -1, features // n_fsdp) for name in some]
        return jnp.concatenate(joined, axis=1)

    for l in reversed(range(layers)):

        def emit(name, delta, values, l=l):
            begun[l, name] = gradient_start(delta, values)

        def gate(point, value, l=l):
            held = ()
            if l == layers - 1:
                if point == "project":
                    held = second(l, ("down", "up"), value)
            elif point == "hidden":
                held = second(l + 1, ("out", "qkv"), value)
                finish(l + 1, ("down", "up"), value)
                along[l + 1] = [along_tp(l + 1, names[:2])]
            elif point == "attend":
                finish(l + 1, ("out", "qkv"), value)
                along[l + 1].append(along_tp(l + 1, names[2:]))
            elif point == "project":
                held = second(l, ("down", "up", "out"), value)
                held += (output, along[l + 1][0], found[l + 1, "out"], found[l + 1, "qkv"])
            elif point == "normed":
                finish(l, ("down",), value)
            return after(value, *held)

        gradient, sums[l] = backward_layer(gradient, saved[l], weights[l], vectors[l], emit, gate)
    local_grad = give_back(gradient)
    second(0, names[3:], local_grad)
    finish(0, names[1:], local_grad)
    pieces = [scatter_pairs(reduced(0, some)) for some in (names[:1], names[1:2], names[2:])]
    mine = [jnp.concatenate(pieces, axis=0)] + [
        after(jnp.concatenate(along[l], axis=0), local_grad) for l in range(1, layers)
    ]
    input_grad = to_all(after(local_grad, *along[1]))

    grads = {name: [] for name in names}
    heights = [found[0, name].shape[0] // n_tp for name in names]
    for l in range(layers):
        other = swap(mine[l])
        low = jnp.where(core == 0, mine[l], other)
        high = jnp.where(core == 0, other, mine[l])
        start = 0
        for name, height in zip(names, heights):
            grads[name].append((low[start : start + height], high[start : start + height]))
            start += height
    rows_joined = lambda name: jnp.stack([jnp.concatenate(p, axis=0) for p in grads[name]]).astype(F32)
    turned = lambda name: jnp.stack([jnp.concatenate([h.T for h in p], axis=1) for p in grads[name]]).astype(F32)
    depth = features // n_fsdp
    qkv_grad = jnp.stack(
        [
            jnp.concatenate([jnp.transpose(h.reshape(3, -1, depth), (2, 0, 1)) for h in p], axis=2)
            for p in grads["qkv"]
        ]
    ).astype(F32)

    def from_core(array, count):
        array = array.reshape(layers, count, n_tp, 1, -1)
        mask = (jnp.arange(2) == core)[:, None]
        return jnp.where(mask, array, 0.0).reshape(-1)

    first = (core == 0).astype(F32)
    member = lambda k: jnp.stack([sums[l][k] for l in range(layers)])
    by_feature = jnp.stack([member(k) for k in (1, 3, 4, 5)]).reshape(4 * layers, features) * first
    if order is not None:
        by_feature = lax.dot_general(
            by_feature, order.astype(F32), (((1,), (1,)), ((), ())), precision=lax.Precision.HIGHEST
        )
    joined = [
        from_core(jnp.swapaxes(member(0).reshape(layers, n_tp, 3, -1)[:, :, ::2], 1, 2), 2),
        from_core(member(2)[:, None], 1),
        by_feature.reshape(-1),
    ]
    summed = jnp.concatenate(joined).reshape(-1, 128)
    if square() and n_tp == 4:
        summed = summed + swap(summed)
        summed = summed + send_x(summed)
        summed = summed + send_y(summed)
        summed = summed + lax.ppermute(summed, "tp", [(0, 1), (1, 0), (2, 3), (3, 2)])
        summed = summed + lax.ppermute(summed, "tp", [(0, 2), (2, 0), (1, 3), (3, 1)])
    else:
        summed = lax.psum(summed, ("fsdp", "ctx", "tp"))
    summed = summed.reshape(-1)
    pick = lambda a, i, axis: lax.dynamic_index_in_dim(a, i, axis, keepdims=True)
    ends = (joined[0].size, joined[0].size + joined[1].size)
    qv_grad = pick(pick(summed[: ends[0]].reshape(layers, 2, n_tp, n_fsdp, -1), lane, 2), group, 3)[:, :, :, 0]
    up_grad = pick(pick(summed[ends[0] : ends[1]].reshape(layers, n_tp, n_fsdp, -1), lane, 1), group, 2)[:, :, 0]
    out_shift, down_shift, one, two = pick(summed[ends[1] :].reshape(4, layers, n_fsdp, -1), group, 2)[:, :, 0]
    return (
        output,
        input_grad,
        qkv_grad,
        qv_grad,
        rows_joined("out"),
        out_shift,
        turned("up"),
        up_grad,
        rows_joined("down"),
        down_shift,
        one,
        two,
    )


def solution(mesh):
    in_specs = (
        P("fsdp", "ctx", None),
        P("fsdp", None),
        P("fsdp"),
        P(None, "fsdp", None, "tp"),
        P(None, None, "tp", "fsdp"),
        P(None, "tp", "fsdp"),
        P(None, "fsdp"),
        P(None, "fsdp", "tp"),
        P(None, "tp", "fsdp"),
        P(None, "tp", "fsdp"),
        P(None, "fsdp"),
        P(None, "fsdp"),
        P(None, "fsdp"),
        P("fsdp", "ctx", None),
    )
    out_specs = (
        P("fsdp", "ctx", None),
        P("fsdp", "ctx", None),
        P(None, "fsdp", None, "tp"),
        P(None, None, "tp", "fsdp"),
        P(None, "tp", "fsdp"),
        P(None, "fsdp"),
        P(None, "fsdp", "tp"),
        P(None, "tp", "fsdp"),
        P(None, "tp", "fsdp"),
        P(None, "fsdp"),
        P(None, "fsdp"),
        P(None, "fsdp"),
    )
    return jax.shard_map(shards, mesh=mesh, in_specs=in_specs, out_specs=out_specs, check_vma=False)
```

```python
import jax
import jax.numpy as jnp
from jax import lax
from jax.experimental import pallas as pl
from jax.experimental.pallas import tpu as pltpu
from jax.sharding import PartitionSpec as P

HD = 64
SEQ = 577
BF = jnp.bfloat16
F32 = jnp.float32


def layer_norm(vectors, scaling):
    centre = vectors - jnp.mean(vectors, axis=-1, keepdims=True)
    spread = jnp.mean(centre * centre, axis=-1, keepdims=True)
    return centre * lax.rsqrt(spread + 1e-06) * scaling


def gelu_exact(values):
    return 0.5 * values * (1.0 + lax.erf(values * 0.7071067811865476))


X_PAIRS = [(0, 1), (1, 0), (2, 3), (3, 2)]
Y_PAIRS = [(0, 2), (2, 0), (1, 3), (3, 1)]
BLOCKS = ((0, 0), (0, 1), (1, 1), (2, 0), (1, 0), (3, 0), (3, 1), (2, 1))


def square():
    return lax.axis_size("fsdp") == 4


def order_matrix(features):
    if not square():
        return None
    half = features // 8
    group = lax.axis_index("fsdp")
    starts = jnp.stack([((group ^ other) * 2 + part) * half for other, part in BLOCKS])
    natural = (starts[:, None] + jnp.arange(half)[None]).reshape(-1)
    return (jnp.arange(features)[:, None] == natural[None]).astype(BF)


def send_x(values):
    return lax.ppermute(values, "fsdp", X_PAIRS)


def send_y(values):
    return lax.ppermute(values, "fsdp", Y_PAIRS)


def after(values, *earlier):
    for array in earlier:
        one = lax.slice(array, (0,) * array.ndim, (1,) * array.ndim).reshape(())
        values = values + jnp.minimum(jnp.abs(one.astype(F32)), 0.0).astype(values.dtype)
    return values


def beside(values, *others):
    return lax.optimization_barrier((values,) + others)[0]


def swap(values):
    return lax.ppermute(values, "ctx", [(0, 1), (1, 0)])


def both_cores(partial_sum):
    low = partial_sum.astype(BF)
    return low.astype(F32) + swap(low).astype(F32)


def tp_bits():
    count = lax.axis_size("tp")
    bits = [1 << k for k in reversed(range(count.bit_length() - 1))]
    assert 1 << len(bits) == count
    return [(bit, axis) for axis, bit in enumerate(bits)]


def tp_partner(values, bit):
    return lax.ppermute(values, "tp", [(j, j ^ bit) for j in range(lax.axis_size("tp"))])


def gather_pairs(shard):
    lane, held = lax.axis_index("tp"), shard
    for bit, axis in tp_bits():
        other = tp_partner(held, bit)
        upper = (lane & bit) != 0
        held = jnp.stack([jnp.where(upper, other, held), jnp.where(upper, held, other)], axis=axis)
    return held.reshape((-1,) + shard.shape)


def scatter_pairs(full):
    lane, bits = lax.axis_index("tp"), tp_bits()
    held = full.reshape((2,) * len(bits) + full.shape[1:])
    for bit, axis in reversed(bits):
        mine = jnp.where((lane & bit) != 0, 1, 0)
        take = lambda k: lax.dynamic_index_in_dim(held, k, axis, keepdims=False)
        other = tp_partner(take(1 - mine), bit)
        held = (take(mine).astype(F32) + other.astype(F32)).astype(BF)
    return held


def gather_features(along, previous):
    if not square():
        return [lax.all_gather(along, "fsdp", axis=along.ndim - 1, tiled=True)], ()
    half = along.shape[-1] // 2
    along = after(along, *previous)
    from_x, from_y = send_x(along), send_y(along)
    far_a, far_b = send_y(from_x[..., :half]), send_x(from_y[..., half:])
    pieces = [along, from_x[..., half:], from_y[..., :half], from_x[..., :half], far_a, far_b, from_y[..., half:]]
    return pieces, (from_x, from_y)


def gather_group(along, heights, previous):
    count = lax.axis_size("tp")
    pieces, came = gather_features(along, previous)
    pieces = [piece.reshape(count, -1, piece.shape[-1]) for piece in pieces]
    result, start = [], 0
    for height in heights:
        cut = [piece[:, start : start + height].reshape(count * height, -1) for piece in pieces]
        result.append(jnp.concatenate(cut, axis=1))
        start += height
    return result, came


def gradient_start(delta, values):
    if not square():
        return lax.psum_scatter(mm_tn(delta, values).astype(BF), "fsdp", scatter_dimension=1, tiled=True)
    half = values.shape[1] // 8
    to_x = mm_tn(delta, values[:, 4 * half : 6 * half]).astype(BF)
    from_x = send_x(to_x)
    to_y = mm_tn(delta, values[:, 6 * half :]).astype(BF)
    from_y = send_y(to_y)
    return mm_tn(delta, values[:, : 4 * half]).astype(BF), from_x, from_y


def gradient_second(begun, marker, hold):
    if not square():
        return begun
    kept, from_x, from_y = begun
    half = from_x.shape[1] // 2
    from_x, from_y = hold(from_x, marker), hold(from_y, marker)
    own_a, own_b, x_b, y_a = jnp.split(kept, 4, axis=1)
    last_a = send_y(y_a + from_x[:, half:])
    last_b = send_x(x_b + from_y[:, :half])
    return (own_a, from_x[:, :half], last_a), (own_b, from_y[:, half:], last_b)


def gradient_finish(terms, marker, hold):
    if not square():
        return terms
    last_a, last_b = hold(terms[0][2], marker), hold(terms[1][2], marker)
    add = lambda own, near, last: (own.astype(F32) + near.astype(F32) + last.astype(F32)).astype(BF)
    return jnp.concatenate([add(*terms[0][:2], last_a), add(*terms[1][:2], last_b)], axis=1)


def mm(left, right):
    return jnp.dot(left, right, preferred_element_type=F32)


def mm_nt(left, right):
    return lax.dot_general(left, right, (((1,), (1,)), ((), ())), preferred_element_type=F32)


def mm_tn(left, right):
    return lax.dot_general(left, right, (((0,), (0,)), ((), ())), preferred_element_type=F32)


def head_scores(project_ref, tile, head):
    part = lambda k: project_ref[:, k * tile + head * HD : k * tile + (head + 1) * HD]
    queries, keys, values = part(0), part(1), part(2)
    scores = mm_nt(queries * BF(HD ** (-0.5)), keys)
    valid = lax.broadcasted_iota(jnp.int32, (1, scores.shape[1]), 1) < SEQ
    return queries, keys, values, jnp.where(valid, scores, -1000000000.0)


def attend_kernel(project_ref, mixed_ref, total_ref):
    tile = mixed_ref.shape[1]
    mixed, totals = [], []
    for head in range(tile // HD):
        values, scores = head_scores(project_ref, tile, head)[2:]
        highest = jnp.max(scores, axis=1, keepdims=True)
        exponent = jnp.exp(scores - highest)
        denominator = jnp.sum(exponent, axis=1, keepdims=True)
        mixed.append(mm(exponent.astype(BF), values) / denominator)
        totals.append(highest + jnp.log(denominator))
    mixed_ref[...] = jnp.concatenate(mixed, axis=1).astype(BF)
    total_ref[0] = jnp.concatenate(totals, axis=1)


def attend_back_kernel(project_ref, mixed_ref, total_ref, delta_ref, out_ref):
    tile = mixed_ref.shape[1]
    scale = HD ** (-0.5)
    parts = ([], [], [])
    for head in range(tile // HD):
        queries, keys, values, scores = head_scores(project_ref, tile, head)
        here = slice(head * HD, (head + 1) * HD)
        delta = delta_ref[:, here]
        probs = jnp.exp(scores - total_ref[0, :, head : head + 1])
        inner = jnp.sum(delta.astype(F32) * mixed_ref[:, here].astype(F32), axis=1, keepdims=True)
        delta_scores = (probs * (mm_nt(delta, values) - inner)).astype(BF)
        parts[0].append(mm(delta_scores, keys) * scale)
        parts[1].append(mm_tn(delta_scores, queries) * scale)
        parts[2].append(mm_tn(probs.astype(BF), delta))
    out_ref[...] = jnp.concatenate(parts[0] + parts[1] + parts[2], axis=1).astype(BF)


def attention_specs(rows, tile):
    wide = pl.BlockSpec((rows, 3 * tile), lambda t: (0, t))
    narrow = pl.BlockSpec((rows, tile), lambda t: (0, t))
    totals = pl.BlockSpec((1, rows, tile // HD), lambda t: (t, 0, 0))
    return wide, narrow, totals


def attend(project, tile):
    rows, count = project.shape[0], project.shape[1] // (3 * tile)
    wide, narrow, totals = attention_specs(rows, tile)
    work = rows * rows * tile * count
    return pl.pallas_call(
        attend_kernel,
        grid=(count,),
        in_specs=[wide],
        out_specs=[narrow, totals],
        out_shape=[
            jax.ShapeDtypeStruct((rows, tile * count), BF),
            jax.ShapeDtypeStruct((count, rows, tile // HD), F32),
        ],
        compiler_params=pltpu.CompilerParams(vmem_limit_bytes=32 * 1024 * 1024),
        cost_estimate=pl.CostEstimate(flops=16 * work, bytes_accessed=8 * project.size // 3, transcendentals=work // HD),
    )(project)


def attend_back(project, mixed, totals, delta, tile):
    rows, count = project.shape[0], project.shape[1] // (3 * tile)
    wide, narrow, per_row = attention_specs(rows, tile)
    work = rows * rows * tile * count
    return pl.pallas_call(
        attend_back_kernel,
        grid=(count,),
        in_specs=[wide, narrow, per_row, narrow],
        out_specs=wide,
        out_shape=jax.ShapeDtypeStruct(project.shape, BF),
        compiler_params=pltpu.CompilerParams(vmem_limit_bytes=32 * 1024 * 1024),
        cost_estimate=pl.CostEstimate(flops=40 * work, bytes_accessed=5 * project.size, transcendentals=work // HD),
    )(project, mixed, totals, delta)


def forward_layer(stream, weights, vectors, gates):
    qkv, out, up, down = weights
    qkv_shift, out_shift, up_shift, down_shift, gain_first, gain_second = vectors
    normed = layer_norm(stream, gain_first).astype(BF)
    project = (mm_nt(normed, qkv) + qkv_shift).astype(BF)
    tile = project.shape[1] // (3 * lax.axis_size("tp"))
    mixed, totals = attend(after(project, *gates[0]), tile)
    mixed = after(mixed, *gates[1])
    middle = stream + both_cores(mm(mixed, out)) + out_shift
    normed_b = layer_norm(middle, gain_second).astype(BF)
    hidden = mm_nt(normed_b, up) + up_shift
    active = gelu_exact(hidden).astype(BF)
    following = middle + both_cores(mm(active, down)) + down_shift
    return following, (stream, normed, project, totals, mixed, middle, normed_b, hidden, active)


def backward_layer(gradient, saved, weights, vectors, emit, gate):
    qkv, out, up, down = weights
    gain_first, gain_second = vectors[4:]
    stream, normed, project, totals, mixed, middle, normed_b, hidden, active = saved
    total = lambda array: jnp.sum(array.astype(F32), axis=0)
    grad_low = gradient.astype(BF)
    emit("down", active, grad_low)
    delta_hidden = jax.vjp(gelu_exact, hidden)[1](mm_nt(grad_low, down))[0].astype(BF)
    delta_hidden = gate("hidden", delta_hidden)
    emit("up", delta_hidden, normed_b)
    delta_normed_b = both_cores(mm(delta_hidden, up))
    back_middle, delta_gain_second = jax.vjp(layer_norm, middle, gain_second)[1](delta_normed_b)
    grad_middle = gradient + back_middle
    grad_attend = grad_middle.astype(BF)
    grad_attend = gate("attend", grad_attend)
    emit("out", mixed, grad_attend)
    delta_mixed = gate("mixed", mm_nt(grad_attend, out).astype(BF))
    tile = mixed.shape[1] // lax.axis_size("tp")
    delta_project = attend_back(project, mixed, totals, delta_mixed, tile)
    delta_project = gate("project", delta_project)
    low = mm(delta_project, qkv).astype(BF)
    emit("qkv", after(delta_project, low), normed)
    delta_normed = gate("normed", low.astype(F32) + swap(low).astype(F32))
    back_stream, delta_gain_first = jax.vjp(layer_norm, stream, gain_first)[1](delta_normed)
    sums = (
        total(delta_project),
        total(grad_attend),
        total(delta_hidden),
        total(grad_low),
        delta_gain_first,
        delta_gain_second,
    )
    return grad_middle + back_stream, sums


def shards(
    tokens,
    lengths,
    image_count,
    qkv_weight,
    qv_bias,
    out_weight,
    out_bias,
    up_weight,
    up_bias,
    down_weight,
    down_bias,
    gain_one,
    gain_two,
    cotangent,
):
    slots, capacity, features = tokens.shape
    layers = qkv_weight.shape[0]
    n_fsdp, n_tp = lax.axis_size("fsdp"), lax.axis_size("tp")
    assert lax.axis_size("ctx") == 2 and slots <= n_tp
    group, core, lane = lax.axis_index("fsdp"), lax.axis_index("ctx"), lax.axis_index("tp")
    rows = -(-SEQ // 16) * 16
    slot = jnp.minimum(lane, slots - 1)
    own_lengths = lax.dynamic_index_in_dim(lengths, slot, 0, keepdims=False)
    live = lane < jnp.minimum(image_count[0], slots)
    row_mask = ((jnp.arange(rows) < SEQ) & live).astype(F32)[:, None]
    halves = lambda array, axis: lax.dynamic_index_in_dim(
        array.reshape(array.shape[:axis] + (2, -1) + array.shape[axis + 1 :]), core, axis, keepdims=False
    )

    cut = []
    for l in range(layers):
        qkv = jnp.transpose(halves(qkv_weight[l], 2), (1, 2, 0)).reshape(-1, qkv_weight.shape[1])
        cut.append((qkv, halves(out_weight[l], 0), halves(up_weight[l], 1).T, halves(down_weight[l], 0)))
    heights = [piece.shape[0] for piece in cut[0]]
    joined = lambda l, members: jnp.concatenate([cut[l][k] for k in members], axis=0)
    stages, along = [], ()
    for l in range(layers):
        for members in ((0, 1), (2,), (3,)) if l else ((0,), (1, 2), (3,)):
            gathered = gather_pairs(after(joined(l, members), *along))
            along = (gathered,)
            stages.append((l, members, gathered.reshape(-1, gathered.shape[-1])))
    first_along = stages[0][2]

    pieces = (qv_bias, up_bias, out_bias, down_bias, gain_one, gain_two)
    packed = jnp.concatenate([piece.reshape(1, -1) for piece in pieces], axis=1)
    if square():
        near_x, near_y = send_x(packed), send_y(packed)
        found = jnp.concatenate([packed, near_x, near_y, send_y(near_x)])
        natural = [lax.dynamic_index_in_dim(found, group ^ k, 0, keepdims=False) for k in range(4)]
        spread = jnp.stack(natural)
    else:
        spread = lax.all_gather(packed[0], "fsdp", axis=0)
    order = order_matrix(features)
    split = qv_bias.size + up_bias.size
    across = gather_pairs(after(spread[:, :split], first_along))

    def by_core(array, count):
        array = array.reshape(n_tp, n_fsdp, layers, count, -1)
        array = jnp.transpose(array, (2, 3, 0, 1, 4)).reshape(layers, count, n_tp, 2, -1)
        return lax.dynamic_index_in_dim(array, core, 3, keepdims=False).reshape(layers, count, -1)

    qv_all = by_core(across[:, :, : qv_bias.size], 2)
    up_all = by_core(across[:, :, qv_bias.size :], 1)
    by_feature = jnp.transpose(spread[:, split:].reshape(n_fsdp, 4, layers, -1), (1, 2, 0, 3)).reshape(4 * layers, features)
    if order is not None:
        by_feature = mm(by_feature, order)
    by_feature = by_feature.astype(F32).reshape(4, layers, features)
    out_all, down_all, one_all, two_all = by_feature[0], by_feature[1], by_feature[2], by_feature[3]
    q_part, v_part = [qv_all[:, k].reshape(layers, n_tp, -1) for k in range(2)]
    qkv_all = jnp.concatenate([q_part, jnp.zeros_like(q_part), v_part], axis=2).reshape(layers, -1).astype(F32)
    vectors = [
        (qkv_all[l], out_all[l], up_all[l, 0], down_all[l], one_all[l], two_all[l])
        for l in range(layers)
    ]

    own_pair = [lax.dynamic_index_in_dim(a, slot, 0, keepdims=False) for a in (tokens, cotangent)]
    own_pair = jnp.concatenate(own_pair, axis=1)
    pair = jnp.concatenate([own_pair, swap(own_pair)], axis=0)
    row = jnp.arange(rows)
    in_first = row < own_lengths[0]
    position = jnp.where(in_first, row, row - own_lengths[0])
    source = position + capacity * (jnp.where(in_first, 0, 1) != core)
    pick_rows = ((jnp.arange(2 * capacity)[None] == source[:, None]) & (row < SEQ)[:, None]).astype(BF)
    packed_pair = mm(pick_rows, pair).astype(BF)
    image = [packed_pair[:, :features], packed_pair[:, features:]]
    if order is not None:
        image = [mm(half, order) for half in image]
    stream = image[0].astype(F32)
    gradient = image[1].astype(F32) * row_mask

    weights = [[] for l in range(layers)]
    came, arrivals = (), []
    for l, members, along in stages:
        more, came = gather_group(along, [heights[k] for k in members], came)
        weights[l] += more
        arrivals.append(came)

    arrivals = [came + (along,) for came, along in zip(arrivals, [stage[2] for stage in stages[1:]] + [()])]
    arrivals = [tuple(jax.tree.leaves(came)) for came in arrivals] + [(), ()]
    saved = []
    for l in range(layers):
        stream, items = forward_layer(stream, weights[l], vectors[l], arrivals[3 * l + 1 : 3 * l + 4])
        saved.append(items)

    place = jnp.arange(capacity)
    target = place + jnp.where(core == 0, 0, own_lengths[0])
    pick_back = (row[None] == target[:, None]) & ((place < own_lengths[core]) & live)[:, None]
    pick_back = pick_back.astype(BF)

    def give_back(values):
        values = values.astype(BF)
        if order is not None:
            values = mm_nt(values, order).astype(BF)
        return mm(pick_back, values).astype(BF)

    def to_all(values):
        return lax.all_gather(values, "tp", axis=0)[:slots]

    output = give_back(stream)
    gradient, output = lax.optimization_barrier((gradient, output))
    output = to_all(output)
    names = ("down", "up", "out", "qkv")
    begun, found = {}, {}
    sums = [None] * layers

    further, along = {}, {}

    def second(layer, some, marker, hold=beside):
        held = ()
        for name in some:
            further[layer, name] = gradient_second(begun[layer, name], marker, hold)
            held += begun[layer, name][1:] if square() else ()
        return held

    def finish(layer, some, marker, hold=beside):
        for name in some:
            found[layer, name] = gradient_finish(further[layer, name], marker, hold)

    def along_tp(layer, some):
        return lax.psum_scatter(reduced(layer, some), "tp", scatter_dimension=0, tiled=False)

    def reduced(layer, some):
        joined = [found[layer, name].reshape(n_tp, -1, features // n_fsdp) for name in some]
        return jnp.concatenate(joined, axis=1)

    for l in reversed(range(layers)):

        def emit(name, delta, values, l=l):
            begun[l, name] = gradient_start(delta, values)

        def gate(point, value, l=l):
            held = ()
            if l == layers - 1:
                if point == "project":
                    held = second(l, ("down", "up"), value)
            elif point == "hidden":
                held = second(l + 1, ("out", "qkv"), value)
                finish(l + 1, ("down", "up"), value)
                along[l + 1] = [along_tp(l + 1, names[:2])]
            elif point == "attend":
                finish(l + 1, ("out", "qkv"), value)
                along[l + 1].append(along_tp(l + 1, names[2:]))
            elif point == "project":
                held = second(l, ("down", "up", "out"), value)
                held += (output, along[l + 1][0], found[l + 1, "out"], found[l + 1, "qkv"])
            elif point == "normed":
                finish(l, ("down",), value)
            return beside(value, *held)

        gradient, sums[l] = backward_layer(gradient, saved[l], weights[l], vectors[l], emit, gate)
    local_grad = give_back(gradient)
    def from_core(array, count):
        array = array.reshape(layers, count, n_tp, 1, -1)
        mask = (jnp.arange(2) == core)[:, None]
        return jnp.where(mask, array, 0.0).reshape(-1)

    first = (core == 0).astype(F32)
    member = lambda k: jnp.stack([sums[l][k] for l in range(layers)])
    by_feature = jnp.stack([member(k) for k in (1, 3, 4, 5)]).reshape(4 * layers, features) * first
    if order is not None:
        by_feature = lax.dot_general(
            by_feature, order.astype(F32), (((1,), (1,)), ((), ())), precision=lax.Precision.HIGHEST
        )
    joined = [
        from_core(jnp.swapaxes(member(0).reshape(layers, n_tp, 3, -1)[:, :, ::2], 1, 2), 2),
        from_core(member(2)[:, None], 1),
        by_feature.reshape(-1),
    ]
    summed = after(jnp.concatenate(joined), local_grad).reshape(-1, 128)
    if square():
        for bit, _ in tp_bits():
            summed = summed + tp_partner(summed, bit)
        over_tp = summed
        summed = summed + swap(summed)
        summed = summed + send_x(summed)
        summed = summed + send_y(summed)
    else:
        over_tp = summed = lax.psum(summed, ("fsdp", "ctx", "tp"))
    second(0, names[3:], local_grad, after)
    finish(0, names[1:], over_tp, after)
    pieces = [scatter_pairs(reduced(0, some)) for some in (names[:1], names[1:2], names[2:])]
    mine = [jnp.concatenate(pieces, axis=0)] + [
        after(jnp.concatenate(along[l], axis=0), local_grad) for l in range(1, layers)
    ]
    input_grad = to_all(local_grad)

    grads = {name: [] for name in names}
    heights = [found[0, name].shape[0] // n_tp for name in names]
    for l in range(layers):
        other = swap(mine[l])
        low = jnp.where(core == 0, mine[l], other)
        high = jnp.where(core == 0, other, mine[l])
        start = 0
        for name, height in zip(names, heights):
            grads[name].append((low[start : start + height], high[start : start + height]))
            start += height
    rows_joined = lambda name: jnp.stack([jnp.concatenate(p, axis=0) for p in grads[name]]).astype(F32)
    turned = lambda name: jnp.stack([jnp.concatenate([h.T for h in p], axis=1) for p in grads[name]]).astype(F32)
    depth = features // n_fsdp
    qkv_grad = jnp.stack(
        [
            jnp.concatenate([jnp.transpose(h.reshape(3, -1, depth), (2, 0, 1)) for h in p], axis=2)
            for p in grads["qkv"]
        ]
    ).astype(F32)

    summed = summed.reshape(-1)
    pick = lambda a, i, axis: lax.dynamic_index_in_dim(a, i, axis, keepdims=True)
    ends = (joined[0].size, joined[0].size + joined[1].size)
    qv_grad = pick(pick(summed[: ends[0]].reshape(layers, 2, n_tp, n_fsdp, -1), lane, 2), group, 3)[:, :, :, 0]
    up_grad = pick(pick(summed[ends[0] : ends[1]].reshape(layers, n_tp, n_fsdp, -1), lane, 1), group, 2)[:, :, 0]
    out_shift, down_shift, one, two = pick(summed[ends[1] :].reshape(4, layers, n_fsdp, -1), group, 2)[:, :, 0]
    return (
        output,
        input_grad,
        qkv_grad,
        qv_grad,
        rows_joined("out"),
        out_shift,
        turned("up"),
        up_grad,
        rows_joined("down"),
        down_shift,
        one,
        two,
    )


def solution(mesh):
    in_specs = (
        P("fsdp", "ctx", None),
        P("fsdp", None),
        P("fsdp"),
        P(None, "fsdp", None, "tp"),
        P(None, None, "tp", "fsdp"),
        P(None, "tp", "fsdp"),
        P(None, "fsdp"),
        P(None, "fsdp", "tp"),
        P(None, "tp", "fsdp"),
        P(None, "tp", "fsdp"),
        P(None, "fsdp"),
        P(None, "fsdp"),
        P(None, "fsdp"),
        P("fsdp", "ctx", None),
    )
    out_specs = (
        P("fsdp", "ctx", None),
        P("fsdp", "ctx", None),
        P(None, "fsdp", None, "tp"),
        P(None, None, "tp", "fsdp"),
        P(None, "tp", "fsdp"),
        P(None, "fsdp"),
        P(None, "fsdp", "tp"),
        P(None, "tp", "fsdp"),
        P(None, "tp", "fsdp"),
        P(None, "fsdp"),
        P(None, "fsdp"),
        P(None, "fsdp"),
    )
    return jax.shard_map(shards, mesh=mesh, in_specs=in_specs, out_specs=out_specs, check_vma=False)
```

```python
import jax
import jax.numpy as jnp
from jax import lax
from jax.experimental import pallas as pl
from jax.experimental.pallas import tpu as pltpu
from jax.sharding import PartitionSpec as P

HD = 64
SEQ = 577
BF = jnp.bfloat16
F32 = jnp.float32


def layer_norm(vectors, scaling):
    centre = vectors - jnp.mean(vectors, axis=-1, keepdims=True)
    spread = jnp.mean(centre * centre, axis=-1, keepdims=True)
    return centre * lax.rsqrt(spread + 1e-06) * scaling


def gelu_exact(values):
    return 0.5 * values * (1.0 + lax.erf(values * 0.7071067811865476))


X_PAIRS = [(0, 1), (1, 0), (2, 3), (3, 2)]
Y_PAIRS = [(0, 2), (2, 0), (1, 3), (3, 1)]
BLOCKS = ((0, 0), (0, 1), (1, 1), (2, 0), (1, 0), (3, 0), (3, 1), (2, 1))


def square():
    return lax.axis_size("fsdp") == 4


def order_matrix(features):
    if not square():
        return None
    half = features // 8
    group = lax.axis_index("fsdp")
    starts = jnp.stack([((group ^ other) * 2 + part) * half for other, part in BLOCKS])
    natural = (starts[:, None] + jnp.arange(half)[None]).reshape(-1)
    return (jnp.arange(features)[:, None] == natural[None]).astype(BF)


def send_x(values):
    return lax.ppermute(values, "fsdp", X_PAIRS)


def send_y(values):
    return lax.ppermute(values, "fsdp", Y_PAIRS)


def after(values, *earlier):
    for array in earlier:
        one = lax.slice(array, (0,) * array.ndim, (1,) * array.ndim).reshape(())
        values = values + jnp.minimum(jnp.abs(one.astype(F32)), 0.0).astype(values.dtype)
    return values


def beside(values, *others):
    return lax.optimization_barrier((values,) + others)[0]


def swap(values):
    return lax.ppermute(values, "ctx", [(0, 1), (1, 0)])


def both_cores(partial_sum):
    low = partial_sum.astype(BF)
    return low.astype(F32) + swap(low).astype(F32)


def tp_bits():
    count = lax.axis_size("tp")
    bits = [1 << k for k in reversed(range(count.bit_length() - 1))]
    assert 1 << len(bits) == count
    return [(bit, axis) for axis, bit in enumerate(bits)]


def tp_partner(values, bit):
    return lax.ppermute(values, "tp", [(j, j ^ bit) for j in range(lax.axis_size("tp"))])


def gather_pairs(shard):
    lane, held = lax.axis_index("tp"), shard
    for bit, axis in tp_bits():
        other = tp_partner(held, bit)
        upper = (lane & bit) != 0
        held = jnp.stack([jnp.where(upper, other, held), jnp.where(upper, held, other)], axis=axis)
    return held.reshape((-1,) + shard.shape)


def scatter_pairs(full):
    lane, bits = lax.axis_index("tp"), tp_bits()
    held = full.reshape((2,) * len(bits) + full.shape[1:])
    for bit, axis in reversed(bits):
        mine = jnp.where((lane & bit) != 0, 1, 0)
        take = lambda k: lax.dynamic_index_in_dim(held, k, axis, keepdims=False)
        other = tp_partner(take(1 - mine), bit)
        held = (take(mine).astype(F32) + other.astype(F32)).astype(BF)
    return held


def gather_features(along, previous):
    if not square():
        return [lax.all_gather(along, "fsdp", axis=along.ndim - 1, tiled=True)], ()
    half = along.shape[-1] // 2
    along = after(along, *previous)
    from_x, from_y = send_x(along), send_y(along)
    far_a, far_b = send_y(from_x[..., :half]), send_x(from_y[..., half:])
    pieces = [along, from_x[..., half:], from_y[..., :half], from_x[..., :half], far_a, far_b, from_y[..., half:]]
    return pieces, (from_x, from_y)


def gather_group(along, heights, previous):
    count = lax.axis_size("tp")
    pieces, came = gather_features(along, previous)
    pieces = [piece.reshape(count, -1, piece.shape[-1]) for piece in pieces]
    result, start = [], 0
    for height in heights:
        cut = [piece[:, start : start + height].reshape(count * height, -1) for piece in pieces]
        result.append(jnp.concatenate(cut, axis=1))
        start += height
    return result, came


def gradient_start(delta, values):
    if not square():
        return lax.psum_scatter(mm_tn(delta, values).astype(BF), "fsdp", scatter_dimension=1, tiled=True)
    half = values.shape[1] // 8
    to_x = mm_tn(delta, values[:, 4 * half : 6 * half]).astype(BF)
    from_x = send_x(to_x)
    to_y = mm_tn(delta, values[:, 6 * half :]).astype(BF)
    from_y = send_y(to_y)
    return mm_tn(delta, values[:, : 4 * half]).astype(BF), from_x, from_y


def gradient_second(begun, marker, hold):
    if not square():
        return begun
    kept, from_x, from_y = begun
    half = from_x.shape[1] // 2
    from_x, from_y = hold(from_x, marker), hold(from_y, marker)
    own_a, own_b, x_b, y_a = jnp.split(kept, 4, axis=1)
    last_a = send_y(y_a + from_x[:, half:])
    last_b = send_x(x_b + from_y[:, :half])
    return (own_a, from_x[:, :half], last_a), (own_b, from_y[:, half:], last_b)


def gradient_finish(terms, marker, hold):
    if not square():
        return terms
    last_a, last_b = hold(terms[0][2], marker), hold(terms[1][2], marker)
    add = lambda own, near, last: (own.astype(F32) + near.astype(F32) + last.astype(F32)).astype(BF)
    return jnp.concatenate([add(*terms[0][:2], last_a), add(*terms[1][:2], last_b)], axis=1)


def mm(left, right):
    return jnp.dot(left, right, preferred_element_type=F32)


def mm_nt(left, right):
    return lax.dot_general(left, right, (((1,), (1,)), ((), ())), preferred_element_type=F32)


def mm_tn(left, right):
    return lax.dot_general(left, right, (((0,), (0,)), ((), ())), preferred_element_type=F32)


def head_scores(project_ref, tile, head):
    part = lambda k: project_ref[:, k * tile + head * HD : k * tile + (head + 1) * HD]
    queries, keys, values = part(0), part(1), part(2)
    scores = mm_nt(queries * BF(HD ** (-0.5)), keys)
    valid = lax.broadcasted_iota(jnp.int32, (1, scores.shape[1]), 1) < SEQ
    return queries, keys, values, jnp.where(valid, scores, -1000000000.0)


def attend_kernel(project_ref, mixed_ref, total_ref):
    tile = mixed_ref.shape[1]
    mixed, totals = [], []
    for head in range(tile // HD):
        values, scores = head_scores(project_ref, tile, head)[2:]
        highest = jnp.max(scores, axis=1, keepdims=True)
        exponent = jnp.exp(scores - highest)
        denominator = jnp.sum(exponent, axis=1, keepdims=True)
        mixed.append(mm(exponent.astype(BF), values) / denominator)
        totals.append(highest + jnp.log(denominator))
    mixed_ref[...] = jnp.concatenate(mixed, axis=1).astype(BF)
    total_ref[0] = jnp.concatenate(totals, axis=1)


def attend_back_kernel(project_ref, mixed_ref, total_ref, delta_ref, out_ref):
    tile = mixed_ref.shape[1]
    scale = HD ** (-0.5)
    parts = ([], [], [])
    for head in range(tile // HD):
        queries, keys, values, scores = head_scores(project_ref, tile, head)
        here = slice(head * HD, (head + 1) * HD)
        delta = delta_ref[:, here]
        probs = jnp.exp(scores - total_ref[0, :, head : head + 1])
        inner = jnp.sum(delta.astype(F32) * mixed_ref[:, here].astype(F32), axis=1, keepdims=True)
        delta_scores = (probs * (mm_nt(delta, values) - inner)).astype(BF)
        parts[0].append(mm(delta_scores, keys) * scale)
        parts[1].append(mm_tn(delta_scores, queries) * scale)
        parts[2].append(mm_tn(probs.astype(BF), delta))
    out_ref[...] = jnp.concatenate(parts[0] + parts[1] + parts[2], axis=1).astype(BF)


def attention_specs(rows, tile):
    wide = pl.BlockSpec((rows, 3 * tile), lambda t: (0, t))
    narrow = pl.BlockSpec((rows, tile), lambda t: (0, t))
    totals = pl.BlockSpec((1, rows, tile // HD), lambda t: (t, 0, 0))
    return wide, narrow, totals


def attend(project, tile):
    rows, count = project.shape[0], project.shape[1] // (3 * tile)
    wide, narrow, totals = attention_specs(rows, tile)
    work = rows * rows * tile * count
    return pl.pallas_call(
        attend_kernel,
        grid=(count,),
        in_specs=[wide],
        out_specs=[narrow, totals],
        out_shape=[
            jax.ShapeDtypeStruct((rows, tile * count), BF),
            jax.ShapeDtypeStruct((count, rows, tile // HD), F32),
        ],
        compiler_params=pltpu.CompilerParams(vmem_limit_bytes=32 * 1024 * 1024),
        cost_estimate=pl.CostEstimate(flops=16 * work, bytes_accessed=8 * project.size // 3, transcendentals=work // HD),
    )(project)


def attend_back(project, mixed, totals, delta, tile):
    rows, count = project.shape[0], project.shape[1] // (3 * tile)
    wide, narrow, per_row = attention_specs(rows, tile)
    work = rows * rows * tile * count
    return pl.pallas_call(
        attend_back_kernel,
        grid=(count,),
        in_specs=[wide, narrow, per_row, narrow],
        out_specs=wide,
        out_shape=jax.ShapeDtypeStruct(project.shape, BF),
        compiler_params=pltpu.CompilerParams(vmem_limit_bytes=32 * 1024 * 1024),
        cost_estimate=pl.CostEstimate(flops=40 * work, bytes_accessed=5 * project.size, transcendentals=work // HD),
    )(project, mixed, totals, delta)


def forward_layer(stream, weights, vectors, gates):
    qkv, out, up, down = weights
    qkv_shift, out_shift, up_shift, down_shift, gain_first, gain_second = vectors
    normed = layer_norm(stream, gain_first).astype(BF)
    project = (mm_nt(normed, qkv) + qkv_shift).astype(BF)
    tile = project.shape[1] // (3 * lax.axis_size("tp"))
    mixed, totals = attend(after(project, *gates[0]), tile)
    mixed = after(mixed, *gates[1])
    middle = stream + both_cores(mm(mixed, out)) + out_shift
    normed_b = layer_norm(middle, gain_second).astype(BF)
    hidden = mm_nt(normed_b, up) + up_shift
    active = gelu_exact(hidden).astype(BF)
    following = middle + both_cores(mm(active, down)) + down_shift
    return following, (stream, normed, project, totals, mixed, middle, normed_b, hidden, active)


def backward_layer(gradient, saved, weights, vectors, emit, gate):
    qkv, out, up, down = weights
    gain_first, gain_second = vectors[4:]
    stream, normed, project, totals, mixed, middle, normed_b, hidden, active = saved
    total = lambda array: jnp.sum(array.astype(F32), axis=0)
    grad_low = gradient.astype(BF)
    emit("down", active, grad_low)
    delta_hidden = jax.vjp(gelu_exact, hidden)[1](mm_nt(grad_low, down))[0].astype(BF)
    delta_hidden = gate("hidden", delta_hidden)
    emit("up", delta_hidden, normed_b)
    delta_normed_b = both_cores(mm(delta_hidden, up))
    back_middle, delta_gain_second = jax.vjp(layer_norm, middle, gain_second)[1](delta_normed_b)
    grad_middle = gradient + back_middle
    grad_attend = grad_middle.astype(BF)
    grad_attend = gate("attend", grad_attend)
    emit("out", mixed, grad_attend)
    delta_mixed = gate("mixed", mm_nt(grad_attend, out).astype(BF))
    tile = mixed.shape[1] // lax.axis_size("tp")
    delta_project = attend_back(project, mixed, totals, delta_mixed, tile)
    delta_project = gate("project", delta_project)
    low = mm(delta_project, qkv).astype(BF)
    emit("qkv", after(delta_project, low), normed)
    delta_normed = gate("normed", low.astype(F32) + swap(low).astype(F32))
    back_stream, delta_gain_first = jax.vjp(layer_norm, stream, gain_first)[1](delta_normed)
    sums = (
        total(delta_project),
        total(grad_attend),
        total(delta_hidden),
        total(grad_low),
        delta_gain_first,
        delta_gain_second,
    )
    return grad_middle + back_stream, sums


def shards(
    tokens,
    lengths,
    image_count,
    qkv_weight,
    qv_bias,
    out_weight,
    out_bias,
    up_weight,
    up_bias,
    down_weight,
    down_bias,
    gain_one,
    gain_two,
    cotangent,
):
    slots, capacity, features = tokens.shape
    layers = qkv_weight.shape[0]
    n_fsdp, n_tp = lax.axis_size("fsdp"), lax.axis_size("tp")
    assert lax.axis_size("ctx") == 2 and slots <= n_tp
    group, core, lane = lax.axis_index("fsdp"), lax.axis_index("ctx"), lax.axis_index("tp")
    rows = -(-SEQ // 16) * 16
    slot = jnp.minimum(lane, slots - 1)
    own_lengths = lax.dynamic_index_in_dim(lengths, slot, 0, keepdims=False)
    live = lane < jnp.minimum(image_count[0], slots)
    row_mask = ((jnp.arange(rows) < SEQ) & live).astype(F32)[:, None]
    halves = lambda array, axis: lax.dynamic_index_in_dim(
        array.reshape(array.shape[:axis] + (2, -1) + array.shape[axis + 1 :]), core, axis, keepdims=False
    )

    cut = []
    for l in range(layers):
        qkv = jnp.transpose(halves(qkv_weight[l], 2), (1, 2, 0)).reshape(-1, qkv_weight.shape[1])
        cut.append((qkv, halves(out_weight[l], 0), halves(up_weight[l], 1).T, halves(down_weight[l], 0)))
    heights = [piece.shape[0] for piece in cut[0]]
    joined = lambda l, members: jnp.concatenate([cut[l][k] for k in members], axis=0)
    stages, along = [], ()
    for l in range(layers):
        for members in ((0, 1), (2,), (3,)) if l else ((0,), (1, 2), (3,)):
            gathered = gather_pairs(after(joined(l, members), *along))
            along = (gathered,)
            stages.append((l, members, gathered.reshape(-1, gathered.shape[-1])))
    first_along = stages[0][2]

    pieces = (qv_bias, up_bias, out_bias, down_bias, gain_one, gain_two)
    packed = jnp.concatenate([piece.reshape(1, -1) for piece in pieces], axis=1)
    if square():
        near_x, near_y = send_x(packed), send_y(packed)
        found = jnp.concatenate([packed, near_x, near_y, send_y(near_x)])
        natural = [lax.dynamic_index_in_dim(found, group ^ k, 0, keepdims=False) for k in range(4)]
        spread = jnp.stack(natural)
    else:
        spread = lax.all_gather(packed[0], "fsdp", axis=0)
    order = order_matrix(features)
    split = qv_bias.size + up_bias.size
    across = gather_pairs(after(spread[:, :split], first_along))

    def by_core(array, count):
        array = array.reshape(n_tp, n_fsdp, layers, count, -1)
        array = jnp.transpose(array, (2, 3, 0, 1, 4)).reshape(layers, count, n_tp, 2, -1)
        return lax.dynamic_index_in_dim(array, core, 3, keepdims=False).reshape(layers, count, -1)

    qv_all = by_core(across[:, :, : qv_bias.size], 2)
    up_all = by_core(across[:, :, qv_bias.size :], 1)
    by_feature = jnp.transpose(spread[:, split:].reshape(n_fsdp, 4, layers, -1), (1, 2, 0, 3)).reshape(4 * layers, features)
    if order is not None:
        by_feature = mm(by_feature, order)
    by_feature = by_feature.astype(F32).reshape(4, layers, features)
    out_all, down_all, one_all, two_all = by_feature[0], by_feature[1], by_feature[2], by_feature[3]
    q_part, v_part = [qv_all[:, k].reshape(layers, n_tp, -1) for k in range(2)]
    qkv_all = jnp.concatenate([q_part, jnp.zeros_like(q_part), v_part], axis=2).reshape(layers, -1).astype(F32)
    vectors = [
        (qkv_all[l], out_all[l], up_all[l, 0], down_all[l], one_all[l], two_all[l])
        for l in range(layers)
    ]

    own_pair = [lax.dynamic_index_in_dim(a, slot, 0, keepdims=False) for a in (tokens, cotangent)]
    own_pair = jnp.concatenate(own_pair, axis=1)
    pair = jnp.concatenate([own_pair, swap(own_pair)], axis=0)
    row = jnp.arange(rows)
    in_first = row < own_lengths[0]
    position = jnp.where(in_first, row, row - own_lengths[0])
    source = position + capacity * (jnp.where(in_first, 0, 1) != core)
    pick_rows = ((jnp.arange(2 * capacity)[None] == source[:, None]) & (row < SEQ)[:, None]).astype(BF)
    packed_pair = mm(pick_rows, pair).astype(BF)
    image = [packed_pair[:, :features], packed_pair[:, features:]]
    if order is not None:
        image = [mm(half, order) for half in image]
    stream = image[0].astype(F32)
    gradient = image[1].astype(F32) * row_mask

    weights = [[] for l in range(layers)]
    came, arrivals = (), []
    for l, members, along in stages:
        more, came = gather_group(along, [heights[k] for k in members], came)
        weights[l] += more
        arrivals.append(came)

    arrivals = [came + (along,) for came, along in zip(arrivals, [stage[2] for stage in stages[1:]] + [()])]
    arrivals = [tuple(jax.tree.leaves(came)) for came in arrivals] + [(), ()]
    saved = []
    for l in range(layers):
        stream, items = forward_layer(stream, weights[l], vectors[l], arrivals[3 * l + 1 : 3 * l + 4])
        saved.append(items)

    place = jnp.arange(capacity)
    target = place + jnp.where(core == 0, 0, own_lengths[0])
    pick_back = (row[None] == target[:, None]) & ((place < own_lengths[core]) & live)[:, None]
    pick_back = pick_back.astype(BF)

    def give_back(values):
        values = values.astype(BF)
        if order is not None:
            values = mm_nt(values, order).astype(BF)
        return mm(pick_back, values).astype(BF)

    def to_all(values):
        return lax.all_gather(values, "tp", axis=0)[:slots]

    output = give_back(stream)
    gradient, output = lax.optimization_barrier((gradient, output))
    output = to_all(output)
    names = ("down", "up", "out", "qkv")
    begun, found = {}, {}
    sums = [None] * layers

    further, along = {}, {}

    def second(layer, some, marker, hold=beside):
        held = ()
        for name in some:
            further[layer, name] = gradient_second(begun[layer, name], marker, hold)
            held += begun[layer, name][1:] if square() else ()
        return held

    def finish(layer, some, marker, hold=beside):
        for name in some:
            found[layer, name] = gradient_finish(further[layer, name], marker, hold)

    def along_tp(layer, some):
        return lax.psum_scatter(reduced(layer, some), "tp", scatter_dimension=0, tiled=False)

    def reduced(layer, some):
        joined = [found[layer, name].reshape(n_tp, -1, features // n_fsdp) for name in some]
        return jnp.concatenate(joined, axis=1)

    for l in reversed(range(layers)):

        def emit(name, delta, values, l=l):
            begun[l, name] = gradient_start(delta, values)

        def gate(point, value, l=l):
            held = ()
            if l == layers - 1:
                if point == "project":
                    held = second(l, ("down", "up"), value)
            elif point == "hidden":
                held = second(l + 1, ("out", "qkv"), value)
                finish(l + 1, ("down", "up"), value)
                along[l + 1] = [along_tp(l + 1, names[:2])]
            elif point == "attend":
                finish(l + 1, ("out", "qkv"), value)
                along[l + 1].append(along_tp(l + 1, names[2:]))
            elif point == "project":
                held = second(l, ("down", "up", "out"), value)
                held += (output, along[l + 1][0], found[l + 1, "out"], found[l + 1, "qkv"])
            elif point == "normed":
                finish(l, ("down",), value)
            return beside(value, *held)

        gradient, sums[l] = backward_layer(gradient, saved[l], weights[l], vectors[l], emit, gate)
    local_grad = give_back(gradient)
    def from_core(array, count):
        array = array.reshape(layers, count, n_tp, 1, -1)
        mask = (jnp.arange(2) == core)[:, None]
        return jnp.where(mask, array, 0.0).reshape(-1)

    first = (core == 0).astype(F32)
    member = lambda k: jnp.stack([sums[l][k] for l in range(layers)])
    by_feature = jnp.stack([member(k) for k in (1, 3, 4, 5)]).reshape(4 * layers, features) * first
    if order is not None:
        by_feature = lax.dot_general(
            by_feature, order.astype(F32), (((1,), (1,)), ((), ())), precision=lax.Precision.HIGHEST
        )
    joined = [
        from_core(jnp.swapaxes(member(0).reshape(layers, n_tp, 3, -1)[:, :, ::2], 1, 2), 2),
        from_core(member(2)[:, None], 1),
        by_feature.reshape(-1),
    ]
    summed = after(jnp.concatenate(joined), local_grad).reshape(-1, 128)
    if square():
        for bit, _ in tp_bits():
            summed = summed + tp_partner(summed, bit)
        over_tp = summed
        summed = summed + swap(summed)
        summed = summed + send_x(summed)
        summed = summed + send_y(summed)
    else:
        over_tp = summed = lax.psum(summed, ("fsdp", "ctx", "tp"))
    second(0, names[3:], local_grad, after)
    finish(0, names[1:2], local_grad, after)
    finish(0, names[2:], over_tp, after)
    pieces = [scatter_pairs(reduced(0, some)) for some in (names[:1], names[1:2], names[2:])]
    mine = [jnp.concatenate(pieces, axis=0)] + [
        after(jnp.concatenate(along[l], axis=0), local_grad) for l in range(1, layers)
    ]
    input_grad = to_all(local_grad)

    grads = {name: [] for name in names}
    heights = [found[0, name].shape[0] // n_tp for name in names]
    for l in range(layers):
        other = swap(mine[l])
        low = jnp.where(core == 0, mine[l], other)
        high = jnp.where(core == 0, other, mine[l])
        start = 0
        for name, height in zip(names, heights):
            grads[name].append((low[start : start + height], high[start : start + height]))
            start += height
    rows_joined = lambda name: jnp.stack([jnp.concatenate(p, axis=0) for p in grads[name]]).astype(F32)
    turned = lambda name: jnp.stack([jnp.concatenate([h.T for h in p], axis=1) for p in grads[name]]).astype(F32)
    depth = features // n_fsdp
    qkv_grad = jnp.stack(
        [
            jnp.concatenate([jnp.transpose(h.reshape(3, -1, depth), (2, 0, 1)) for h in p], axis=2)
            for p in grads["qkv"]
        ]
    ).astype(F32)

    summed = summed.reshape(-1)
    pick = lambda a, i, axis: lax.dynamic_index_in_dim(a, i, axis, keepdims=True)
    ends = (joined[0].size, joined[0].size + joined[1].size)
    qv_grad = pick(pick(summed[: ends[0]].reshape(layers, 2, n_tp, n_fsdp, -1), lane, 2), group, 3)[:, :, :, 0]
    up_grad = pick(pick(summed[ends[0] : ends[1]].reshape(layers, n_tp, n_fsdp, -1), lane, 1), group, 2)[:, :, 0]
    out_shift, down_shift, one, two = pick(summed[ends[1] :].reshape(4, layers, n_fsdp, -1), group, 2)[:, :, 0]
    return (
        output,
        input_grad,
        qkv_grad,
        qv_grad,
        rows_joined("out"),
        out_shift,
        turned("up"),
        up_grad,
        rows_joined("down"),
        down_shift,
        one,
        two,
    )


def solution(mesh):
    in_specs = (
        P("fsdp", "ctx", None),
        P("fsdp", None),
        P("fsdp"),
        P(None, "fsdp", None, "tp"),
        P(None, None, "tp", "fsdp"),
        P(None, "tp", "fsdp"),
        P(None, "fsdp"),
        P(None, "fsdp", "tp"),
        P(None, "tp", "fsdp"),
        P(None, "tp", "fsdp"),
        P(None, "fsdp"),
        P(None, "fsdp"),
        P(None, "fsdp"),
        P("fsdp", "ctx", None),
    )
    out_specs = (
        P("fsdp", "ctx", None),
        P("fsdp", "ctx", None),
        P(None, "fsdp", None, "tp"),
        P(None, None, "tp", "fsdp"),
        P(None, "tp", "fsdp"),
        P(None, "fsdp"),
        P(None, "fsdp", "tp"),
        P(None, "tp", "fsdp"),
        P(None, "tp", "fsdp"),
        P(None, "fsdp"),
        P(None, "fsdp"),
        P(None, "fsdp"),
    )
    return jax.shard_map(shards, mesh=mesh, in_specs=in_specs, out_specs=out_specs, check_vma=False)
```
